32 devices in a mesh: tm: 4 (over x, core), space: 8 (over z, y).
Axes of the slice: x: 2, y: 2, z: 4, core: 2. Of those that a mesh axis runs over, the one named last changes fastest.
Arguments:
- initial: bfloat16 [135, 1024], P(None, 'space'), may hold values from -6 to 6
- forcing: bfloat16 [64, 135, 1024], P('tm', None, 'space'), may hold values from -2 to 2
- damping: float32 [1024], P('space'), may hold values from 0.003 to 0.1
- block_inv: bfloat16 [2, 135, 135], replicated, as said below
- coarse_inv: bfloat16 [2, 135, 135], replicated, as said below
- coupling: bfloat16 [6, 135, 135], replicated, may hold values from -0.078125 to 0.078125
- etype: int32 [8], P('space'), may hold values from 0 to 1
- send_index: int32 [1024], P('space'), may hold values from 0 to 127
- conn: int32 [6, 1024], P(None, 'space'), may hold values from 0 to 255
Outputs:
- states: bfloat16 [64, 135, 1024], P('tm', None, 'space')
The draws below stay inside these ranges and needn't reach their ends.
Inputs may be any that keep to these rules, and one draw needn't show every extreme that they name: block_inv[0] is the inverse of a hexahedron's diagonal block, block_inv[1] that of a prism, with zero rows and columns from 90 on. coarse_inv[0] is the inverse of a hexahedron's coarse diagonal block, coarse_inv[1] that of a prism, with zero rows and columns from 90 on. `send_index`: the first 64 entries of a partition's list name the elements it sends to the partition before, the last 64 those it sends to the partition after. `conn`: entries below 128 name an element of the same partition; the next 64 name the columns received from the partition before, the last 64 those received from the partition after.
All inputs are finite; a program needn't handle non-finite values.
Results may differ from the reference program's by a relative error of at most 0.018.
Values may be sent and summed in bfloat16 or wider, within the bound.
No kernel may reach another device: no remote copies, remote signals or barrier semaphores. Data moves between devices by JAX's collectives and lax.ppermute only.
A program may use at most 64 MiB of HBM per device.

```python
import math
import jax
import jax.numpy as jnp
from jax import lax

W = 135
PRISM = 90
FACES = 6
SWEEPS = 2
COARSEN = 4
BLK = 128
E_DEV = 128
HALO = 64
STEPS = 64
ELEMS = 1024
NBLK = 8
SEND = 1024
N_SPACE = 8


def make_inverse(key, shift_value, skew_value):
    inverses = []
    for element_kind in range(2):
        used_rows = W if element_kind == 0 else PRISM
        sub_key = jax.random.fold_in(key, element_kind)
        normals = jax.random.normal(sub_key, (W, W), jnp.float32)
        scales = jax.random.uniform(jax.random.fold_in(sub_key, 7), (W,), jnp.float32, 1.0, 1.1)
        inside = jnp.arange(W) < used_rows
        both_inside = inside[:, None] & inside[None, :]
        skewed = jnp.where(both_inside, (normals - normals.T) / jnp.sqrt(2.0 * W), 0.0)
        matrix = shift_value * jnp.diag(scales) + skew_value * skewed
        inverse = jnp.linalg.solve(matrix, jnp.eye(W, dtype=jnp.float32))
        inverses.append(jnp.where(both_inside, inverse, 0.0))
    return jnp.stack(inverses).astype(jnp.bfloat16)


def draw_block_inv(key, part):
    return make_inverse(jax.random.fold_in(key, 11), 1.03, 0.6)


def draw_coarse_inv(key, part):
    return make_inverse(jax.random.fold_in(key, 23), 1.12, 1.6)


def set_ends(array, stream_key, least, largest):
    longest = array.shape.index(max(array.shape))
    spots = []
    for shift in (0, 1):
        where = [jax.random.randint(jax.random.fold_in(stream_key, axis), (), 0, length) for axis, length in enumerate(array.shape)]
        where[longest] = (where[longest] + shift) % array.shape[longest]
        spots.append(tuple(where))
    return array.at[spots[0]].set(least).at[spots[1]].set(largest)


def level_of(key, dims, shards, low, high):
    level = 1.0
    for position, shards_of in shards:
        heights = jax.random.uniform(jax.random.fold_in(jax.random.fold_in(key, 6), position), (shards_of,), jnp.float32, low / len(shards), high / len(shards))
        level = level * jnp.repeat(jnp.exp(heights), dims[position] // shards_of).reshape((-1,) + (1,) * (len(dims) - 1 - position))
    return level


def scatter_about(key, extent, spread, reach, split=(), kind=jnp.bfloat16):
    result = jax.random.normal(key, extent, jnp.float32) * spread
    if len(split) > 0:
        result = level_of(key, extent, split, -0.22, 0.18) * result
    return jnp.clip(result, min=-reach, max=reach).astype(kind)


def setup_inputs(seed: int = 0) -> dict:
    key_of = jax.random.split(jax.random.key(seed), 10)
    initial = scatter_about(key_of[0], (W, ELEMS), 1.0, 6.0, ((1, 8),))
    forcing = scatter_about(key_of[1], (STEPS, W, ELEMS), 0.3, 2.0, ((0, 4), (2, 8)))
    damping = jnp.clip(jnp.exp(math.log(0.1) - 3.506558 * jax.random.uniform(key_of[2], (ELEMS,), jnp.float32) ** level_of(key_of[2], (ELEMS,), ((0, 8),), -0.2, 0.2)), 0.003, 0.1)
    block_inv = draw_block_inv(jax.random.fold_in(key_of[9], 71), 0)
    coarse_inv = draw_coarse_inv(jax.random.fold_in(key_of[9], 71), 0)
    coupling = scatter_about(key_of[5], (FACES, W, W), (40 * W) ** -0.5, 0.078125)
    etype = set_ends(jax.random.randint(key_of[6], (NBLK,), 0, 2), jax.random.fold_in(key_of[6], 1), 0, 1).astype(jnp.int32)
    send_index = set_ends(jax.random.randint(key_of[7], (SEND,), 0, E_DEV), jax.random.fold_in(key_of[7], 1), 0, E_DEV - 1).astype(jnp.int32)
    conn = set_ends(jax.random.randint(key_of[8], (FACES, ELEMS), 0, E_DEV + 2 * HALO), jax.random.fold_in(key_of[8], 1), 0, (E_DEV + 2 * HALO) - 1).astype(jnp.int32)
    return dict(initial=initial, forcing=forcing, damping=damping, block_inv=block_inv, coarse_inv=coarse_inv, coupling=coupling, etype=etype, send_index=send_index, conn=conn)


def face_tables(etype, conn, send_index):
    element_kinds = jnp.repeat(etype, BLK)
    face_rows = lax.broadcasted_iota(jnp.int32, (FACES, ELEMS), 0)
    keep_faces = ((face_rows < FACES - 1) | (element_kinds[None, :] == 0)).astype(jnp.bfloat16)
    keep_parts = keep_faces.reshape(FACES, N_SPACE, E_DEV).transpose(1, 0, 2)
    conn_parts = conn.reshape(FACES, N_SPACE, E_DEV).transpose(1, 0, 2).reshape(N_SPACE, FACES * E_DEV)
    send_parts = send_index.reshape(N_SPACE, 2 * HALO)
    return (element_kinds, (keep_parts, conn_parts, send_parts))

def coupled_term(iterate, coupling, tables):
    keep_parts, conn_parts, send_parts = tables
    pieces = iterate.reshape(W, N_SPACE, E_DEV)
    outgoing = jnp.take_along_axis(pieces, jnp.broadcast_to(send_parts[None], (W, N_SPACE, 2 * HALO)), axis=2)
    zero_rim = jnp.zeros((W, 1, HALO), jnp.bfloat16)
    from_before = jnp.concatenate([zero_rim, outgoing[:, :-1, HALO:]], axis=1)
    from_after = jnp.concatenate([outgoing[:, 1:, :HALO], zero_rim], axis=1)
    extended = jnp.concatenate([pieces, from_before, from_after], axis=2)
    gathered = jnp.take_along_axis(extended, jnp.broadcast_to(conn_parts[None], (W, N_SPACE, FACES * E_DEV)), axis=2)
    gathered = gathered.reshape(W, N_SPACE, FACES, E_DEV) * keep_parts[None]
    summed = jnp.einsum('fij,jpfk->ipk', coupling.astype(jnp.float32), gathered.astype(jnp.float32))
    return summed.reshape(W, ELEMS)

def apply_inverse(rhs_value, chosen):
    blocked = rhs_value.reshape(W, NBLK, BLK)
    applied = jnp.einsum('bij,jbk->ibk', chosen.astype(jnp.float32), blocked.astype(jnp.float32))
    return applied.reshape(W, ELEMS)

def propagate(start_state, drive_term, chosen, coupling, tables):
    iterate = start_state
    for sweep_index in range(SWEEPS):
        coupled = coupled_term(iterate, coupling, tables)
        rhs_value = (drive_term - coupled).astype(jnp.bfloat16)
        iterate = apply_inverse(rhs_value, chosen).astype(jnp.bfloat16)
    return iterate

def reference(initial, forcing, damping, block_inv, coarse_inv, coupling, etype, send_index, conn):
    element_kinds, tables = face_tables(etype, conn, send_index)
    is_hex = (etype == 0)[:, None, None]
    fine_chosen = jnp.where(is_hex, block_inv[0][None], block_inv[1][None])
    coarse_chosen = jnp.where(is_hex, coarse_inv[0][None], coarse_inv[1][None])
    rows_iota = lax.broadcasted_iota(jnp.int32, (W, ELEMS), 0)
    valid_rows = (rows_iota < PRISM) | (element_kinds[None, :] == 0)
    start_field = jnp.where(valid_rows, initial, jnp.zeros_like(initial))
    decay_rate = jnp.exp(-damping)
    coarse_decay = jnp.exp(-COARSEN * damping)
    intervals = STEPS // COARSEN
    forcing_view = forcing.reshape(intervals, COARSEN, W, ELEMS)

    def fine_step(states_now, forcing_now):

        def single(paired):
            drive_term = decay_rate[None, :] * paired[0].astype(jnp.float32) + paired[1].astype(jnp.float32)
            return propagate(paired[0], drive_term, fine_chosen, coupling, tables)
        return lax.map(single, (states_now, forcing_now))
    zero_rest = jnp.zeros((intervals - 1, W, ELEMS), jnp.bfloat16)
    states_now = jnp.concatenate([start_field[None], zero_rest], axis=0)
    for step_index in range(COARSEN):
        states_now = fine_step(states_now, forcing_view[:, step_index])
    residuals = states_now

    def coarse_advance(carried, residual_now):
        drive_term = coarse_decay[None, :] * carried.astype(jnp.float32)
        propagated = propagate(carried, drive_term, coarse_chosen, coupling, tables)
        advanced = (propagated.astype(jnp.float32) + residual_now.astype(jnp.float32)).astype(jnp.bfloat16)
        return (advanced, advanced)
    _, coarse_values = lax.scan(coarse_advance, jnp.zeros((W, ELEMS), jnp.bfloat16), residuals)
    states_now = jnp.concatenate([start_field[None], coarse_values[:-1]], axis=0)
    produced = []
    for step_index in range(COARSEN - 1):
        states_now = fine_step(states_now, forcing_view[:, step_index])
        produced.append(states_now)
    produced.append(coarse_values)
    return jnp.stack(produced, axis=1).reshape(STEPS, W, ELEMS)
```

```python
import functools

import jax
import jax.numpy as jnp
from jax import lax
from jax.experimental import pallas as pl
from jax.experimental.pallas import tpu as pltpu
from jax.sharding import PartitionSpec as P

PRISM = 90
SWEEPS = 2
COARSEN = 4
ROWS = 144
PROWS = 96
LANES = 128
BF = jnp.bfloat16
F32 = jnp.float32
VMEM = pl.BlockSpec(memory_space=pltpu.VMEM)
LIMIT = 56 * 1024 * 1024


def dot(a, b):
    return jnp.dot(a, b, preferred_element_type=F32)


def host_of(window, interval, space, intervals):
    stride = space // intervals
    return (interval * stride + (window % 2) % stride) % space


class Place:
    def __init__(self, space, intervals):
        stride = space // intervals
        self.window = lax.axis_index("tm")
        self.position = lax.axis_index("space")
        shifted = lax.rem(
            self.position - lax.rem(lax.rem(self.window, 2), stride) + space, space
        )
        self.active = lax.rem(shifted, stride) == 0
        self.interval = shifted // stride
        self.next_interval = lax.rem((shifted + stride - 1) // stride, intervals)
        self.number = self.window * intervals + self.interval


def over_pairs(parts, body):
    if parts <= 8:
        for pair in range(parts // 2):
            body(pair)
    else:

        @pl.loop(0, parts // 2)
        def _(pair):
            body(pair)


class Sweeper:
    def __init__(self, parts, faces, gather, listing, aux, outs, work):
        self.parts, self.faces = parts, faces
        self.gather, self.listing, self.aux = gather, listing, aux
        self.outs, self.work = outs, work

    def clear_rim(self):
        zero = jnp.zeros((ROWS, LANES), BF)
        self.outs[0] = zero
        self.outs[self.parts + 1] = zero

    def set_drive(self, state, decay_row, forcing=None):
        def body(pair):
            for side in range(2):
                part = 2 * pair + side
                drive = state[part].astype(F32) * self.aux[part, decay_row : decay_row + 1, :]
                if forcing is not None:
                    drive = drive + forcing(part).astype(F32)
                self.work[
                    pair, self.faces * ROWS :, side * LANES : (side + 1) * LANES
                ] = drive.astype(BF)

        over_pairs(self.parts, body)

    def sweep(self, source, target, table, extra=None):
        lane = lax.broadcasted_iota(jnp.int32, (ROWS, LANES), 1)

        def listed(pair):
            both = jnp.concatenate([source[2 * pair], source[2 * pair + 1]], axis=1)
            chosen = dot(both, self.listing[pair]).astype(BF)
            self.outs[2 * pair + 1] = chosen[:, :LANES]
            self.outs[2 * pair + 2] = chosen[:, LANES:]

        def gathered(pair):
            for side in range(2):
                part = 2 * pair + side
                rim = jnp.where(lane < LANES // 2, self.outs[part], self.outs[part + 2])
                extended = jnp.concatenate([source[part], rim], axis=1)
                found = dot(extended, self.gather[part]).astype(BF)
                for face in range(self.faces):
                    self.work[
                        pair,
                        face * ROWS : (face + 1) * ROWS,
                        side * LANES : (side + 1) * LANES,
                    ] = found[:, face * LANES : (face + 1) * LANES]

        def applied(pair):
            both = dot(table[...], self.work[pair])
            for side in range(2):
                part = 2 * pair + side
                result = both[:, side * LANES : (side + 1) * LANES]
                prism = jnp.concatenate(
                    [result[ROWS:], jnp.zeros((ROWS - PROWS, LANES), F32)], axis=0
                )
                kind = self.aux[part, 0:1, :]
                value = jnp.where(kind == 0.0, result[:ROWS], prism)
                if extra is not None:
                    value = value + extra[part].astype(F32)
                target[part] = value.astype(BF)

        over_pairs(self.parts, listed)
        over_pairs(self.parts, gathered)
        over_pairs(self.parts, applied)

    def step(self, state, other, table, decay_row, forcing=None, extra=None):
        self.set_drive(state, decay_row, forcing)
        places = [state, other]
        for turn in range(SWEEPS):
            last = turn + 1 == SWEEPS
            self.sweep(
                places[turn % 2], places[(turn + 1) % 2], table, extra if last else None
            )


def pack_kernel(space, intervals, forcing, initial, meta, *messages):
    place = Place(space, intervals)
    width = initial.shape[0]
    for turn in range(intervals):
        interval = lax.rem(place.next_interval + turn, intervals)
        out = messages[turn]
        for index in range(COARSEN):
            out[index, :width] = forcing[interval * COARSEN + index]
        out[COARSEN, :width] = initial[...]
        out[0, width : width + 8] = meta[0:8]
        out[1, width : width + 3] = meta[8:11]


def fine_kernel(space, intervals, width, faces, *refs):
    messages = refs[:space]
    table, residual, gather, listing, aux, forcing, start = refs[space : space + 7]
    other, outs, work = refs[space + 7 :]
    place = Place(space, intervals)

    @pl.when(place.active)
    def _():
        sweeper = Sweeper(space, faces, gather, listing, aux, outs, work)
        sweeper.clear_rim()
        rows = lax.broadcasted_iota(jnp.int32, (ROWS, LANES), 0).astype(F32)
        full = lax.broadcasted_iota(jnp.int32, (2 * LANES, LANES), 0).astype(F32)
        half = full[:LANES]
        zero = jnp.zeros((LANES, LANES), BF)
        for turn in range(space):
            part = lax.rem(place.position - turn + space, space)
            message = messages[turn]
            for index in range(COARSEN):
                forcing[part, index] = message[index]
            first = message[0, width : width + 8].astype(F32)
            second = message[1, width : width + 3].astype(F32)
            kind = first[6:7]
            damping = (second[0:1] + second[1:2]) + second[2:3]
            aux[part] = jnp.concatenate(
                [
                    kind,
                    jnp.exp(-damping),
                    jnp.exp(-COARSEN * damping),
                    jnp.zeros((5, LANES), F32),
                ],
                axis=0,
            )
            for face in range(faces):
                found = full == first[face : face + 1]
                if face == faces - 1:
                    found = found & (kind == 0.0)
                gather[part, :, face * LANES : (face + 1) * LANES] = jnp.where(
                    found, 1.0, 0.0
                ).astype(BF)
            picks = jnp.where(half == first[7:8], 1.0, 0.0).astype(BF)
            odd = lax.rem(part, 2) == 1
            left = jnp.where(odd, 0.0, 1.0).astype(BF)
            right = jnp.where(odd, 1.0, 0.0).astype(BF)
            listing[part // 2, pl.ds(pl.multiple_of(lax.rem(part, 2) * LANES, LANES), LANES), :] = (
                jnp.concatenate([picks * left, picks * right], axis=1)
            )
            limit = jnp.where(kind == 0.0, float(width), float(PRISM))
            wanted = (rows < limit) & (place.number == 0)
            start[part] = jnp.where(wanted, message[COARSEN].astype(F32), 0.0).astype(BF)

        residual[...] = start[...]

        @pl.loop(0, COARSEN)
        def _(index):
            sweeper.step(residual, other, table, 1, lambda part: forcing[part, index])


def chain_kernel(space, intervals, faces, powers, count, *refs):
    terms = refs[:count]
    table, gather, listing, aux, result, other, outs, work = refs[count:]
    place = Place(space, intervals)

    @pl.when(place.active)
    def _():
        sweeper = Sweeper(space, faces, gather, listing, aux, outs, work)
        sweeper.clear_rim()
        result[...] = terms[0][...]
        for index in range(1, count):
            if powers > 1:

                @pl.loop(0, powers - 1)
                def _(turn):
                    sweeper.step(result, other, table, 2)

            sweeper.step(result, other, table, 2, extra=terms[index])


def final_kernel(space, intervals, width, faces, *refs):
    before, residual, start, forcing = refs[:4]
    fine_table, coarse_table, gather, listing, aux = refs[4:9]
    pieces = refs[9 : 9 + space]
    states, other, outs, work = refs[9 + space :]
    place = Place(space, intervals)

    @pl.when(place.active)
    def _():
        sweeper = Sweeper(space, faces, gather, listing, aux, outs, work)
        sweeper.clear_rim()
        last = COARSEN - 1
        state = states.at[last]
        state[...] = before[...]
        sweeper.step(state, other, coarse_table, 2, extra=residual)
        first = place.number == 0
        states[0] = jnp.where(first, start[...], before[...])

        @pl.loop(0, last)
        def _(index):
            now = states.at[index]
            sweeper.step(now, other, fine_table, 1, lambda part: forcing[part, index])

            @pl.when(index + 1 < last)
            def _():
                states[index + 1] = now[...]

        for turn in range(space):
            part = lax.rem(place.position + turn, space)
            for index in range(COARSEN):
                pieces[turn][index] = states[index, part][:width]


def gather_kernel(space, intervals, *refs):
    pieces = refs[:space]
    out, sem = refs[space:]
    stride = space // intervals
    place = Place(space, intervals)
    offset = lax.rem(lax.rem(place.window, 2), stride)
    for interval in range(intervals):
        wanted = lax.rem(place.position - offset - interval * stride + 2 * space, space)
        for turn in range(space):

            @pl.when(wanted == turn)
            def _():
                pltpu.make_async_copy(
                    pieces[turn], out.at[pl.ds(interval * COARSEN, COARSEN)], sem.at[interval]
                ).start()

    for interval in range(intervals):
        pltpu.make_async_copy(
            pieces[0], out.at[pl.ds(interval * COARSEN, COARSEN)], sem.at[interval]
        ).wait()


def folded(inverse, coupling):
    width = inverse.shape[-1]
    faces = coupling.shape[0]
    products = -jnp.einsum("kij,fjl->kifl", inverse, coupling, preferred_element_type=F32)
    every = jnp.concatenate([products.astype(BF), inverse[:, :, None, :]], axis=2)
    every = jnp.pad(every, ((0, 0), (0, 0), (0, 0), (0, ROWS - width)))
    every = every.reshape(2, width, (faces + 1) * ROWS)
    return jnp.concatenate(
        [
            jnp.pad(every[0], ((0, ROWS - width), (0, 0))),
            jnp.pad(every[1, :PRISM], ((0, PROWS - PRISM), (0, 0))),
        ],
        axis=0,
    )


def shards(initial, forcing, damping, block_inv, coarse_inv, coupling, etype, send_index, conn):
    width, elems = initial.shape
    faces = conn.shape[0]
    steps = forcing.shape[0]
    intervals = steps // COARSEN
    space = lax.axis_size("space")
    windows = lax.axis_size("tm")
    stride = space // intervals
    halo = send_index.shape[0] // 2
    params = pltpu.CompilerParams(vmem_limit_bytes=LIMIT)
    state_shape = jax.ShapeDtypeStruct((space, ROWS, LANES), BF)

    kinds = jnp.broadcast_to(etype[:, None], (etype.shape[0], elems // etype.shape[0]))
    lists = jnp.concatenate([send_index[halo:], send_index[:halo]])
    high = lax.reduce_precision(damping, 8, 7)
    middle = lax.reduce_precision(damping - high, 8, 7)
    low = (damping - high) - middle
    meta = jnp.concatenate(
        [
            conn.astype(F32),
            kinds.reshape(1, elems).astype(F32),
            lists[None].astype(F32),
            high[None],
            middle[None],
            low[None],
            jnp.zeros((16 - faces - 5, elems), F32),
        ],
        axis=0,
    ).astype(BF)

    message_shape = jax.ShapeDtypeStruct((COARSEN + 1, ROWS, LANES), BF)
    messages = pl.pallas_call(
        functools.partial(pack_kernel, space, intervals),
        out_shape=[message_shape] * intervals,
        in_specs=[VMEM] * 3,
        out_specs=[VMEM] * intervals,
        compiler_params=params,
        name="pack",
    )(forcing, initial, meta)

    received = [messages[0]]
    for turn in range(1, space):
        pairs = []
        for window in range(windows):
            for interval in range(intervals):
                host = host_of(window, interval, space, intervals)
                source = (host - turn) % space
                pairs.append((window * space + source, window * space + host))
        received.append(lax.ppermute(messages[turn // stride], ("tm", "space"), pairs))

    fine_table = folded(block_inv, coupling)
    coarse_table = folded(coarse_inv, coupling)

    gather_shape = jax.ShapeDtypeStruct((space, 2 * LANES, faces * LANES), BF)
    listing_shape = jax.ShapeDtypeStruct((space // 2, 2 * LANES, 2 * LANES), BF)
    aux_shape = jax.ShapeDtypeStruct((space, 8, LANES), F32)
    forcing_shape = jax.ShapeDtypeStruct((space, COARSEN, ROWS, LANES), BF)
    scratch = [
        pltpu.VMEM((space, ROWS, LANES), BF),
        pltpu.VMEM((space + 2, ROWS, LANES), BF),
        pltpu.VMEM((space // 2, (faces + 1) * ROWS, 2 * LANES), BF),
    ]
    residual, gather, listing, aux, whole_forcing, start = pl.pallas_call(
        functools.partial(fine_kernel, space, intervals, width, faces),
        out_shape=[state_shape, gather_shape, listing_shape, aux_shape, forcing_shape, state_shape],
        in_specs=[VMEM] * (space + 1),
        out_specs=[VMEM] * 6,
        scratch_shapes=scratch,
        compiler_params=params,
        name="fine",
    )(*received, fine_table)

    def from_earlier(value, by):
        pairs = []
        for number in range(by, windows * intervals):
            target = number // intervals
            source = (number - by) // intervals
            pairs.append(
                (
                    source * space + host_of(source, (number - by) % intervals, space, intervals),
                    target * space + host_of(target, number % intervals, space, intervals),
                )
            )
        return lax.ppermute(value, ("tm", "space"), pairs)

    def chain(terms, powers, name):
        return pl.pallas_call(
            functools.partial(chain_kernel, space, intervals, faces, powers, len(terms)),
            out_shape=state_shape,
            in_specs=[VMEM] * (len(terms) + 4),
            out_specs=VMEM,
            scratch_shapes=scratch,
            compiler_params=params,
            name=name,
        )(*terms, coarse_table, gather, listing, aux)

    near = [from_earlier(residual, by) for by in range(intervals, 0, -1)]
    partial = chain(near, 1, "near")
    far = [from_earlier(partial, by * intervals) for by in range(windows - 1, 0, -1)]
    before = chain(far + [partial], intervals, "far")

    piece_shape = jax.ShapeDtypeStruct((COARSEN, width, LANES), BF)
    pieces = pl.pallas_call(
        functools.partial(final_kernel, space, intervals, width, faces),
        out_shape=[piece_shape] * space,
        in_specs=[VMEM] * 9,
        out_specs=[VMEM] * space,
        scratch_shapes=[pltpu.VMEM((COARSEN, space, ROWS, LANES), BF)] + scratch,
        compiler_params=params,
        name="final",
    )(before, residual, start, whole_forcing, fine_table, coarse_table, gather, listing, aux)

    returned = [pieces[0]]
    for turn in range(1, space):
        pairs = []
        for window in range(windows):
            for interval in range(intervals):
                host = host_of(window, interval, space, intervals)
                pairs.append((window * space + host, window * space + (host + turn) % space))
        returned.append(lax.ppermute(pieces[turn], ("tm", "space"), pairs))

    return pl.pallas_call(
        functools.partial(gather_kernel, space, intervals),
        out_shape=jax.ShapeDtypeStruct(forcing.shape, BF),
        in_specs=[pl.BlockSpec(memory_space=pl.ANY)] * space,
        out_specs=pl.BlockSpec(memory_space=pl.ANY),
        scratch_shapes=[pltpu.SemaphoreType.DMA((intervals,))],
        compiler_params=params,
        name="place",
    )(*returned)


def solution(mesh):
    in_specs = (
        P(None, "space"),
        P("tm", None, "space"),
        P("space"),
        P(),
        P(),
        P(),
        P("space"),
        P("space"),
        P(None, "space"),
    )
    out_specs = P("tm", None, "space")
    return jax.shard_map(shards, mesh=mesh, in_specs=in_specs, out_specs=out_specs, check_vma=False)
```

```python
import functools

import jax
import jax.numpy as jnp
from jax import lax
from jax.experimental import pallas as pl
from jax.experimental.pallas import tpu as pltpu
from jax.sharding import PartitionSpec as P

PRISM = 90
SWEEPS = 2
COARSEN = 4
ROWS = 144
PROWS = 96
LANES = 128
BF = jnp.bfloat16
F32 = jnp.float32
VMEM = pl.BlockSpec(memory_space=pltpu.VMEM)
MIB = 1024 * 1024


def dot(a, b):
    return jnp.dot(a, b, preferred_element_type=F32)


def host_of(window, interval, space, intervals):
    stride = space // intervals
    return (interval * stride + (window % 2) % stride) % space


class Place:
    def __init__(self, space, intervals):
        stride = space // intervals
        self.window = lax.axis_index("tm")
        self.position = lax.axis_index("space")
        shifted = lax.rem(
            self.position - lax.rem(lax.rem(self.window, 2), stride) + space, space
        )
        self.active = lax.rem(shifted, stride) == 0
        self.interval = shifted // stride
        self.next_interval = lax.rem((shifted + stride - 1) // stride, intervals)
        self.number = self.window * intervals + self.interval


def over_pairs(parts, body):
    if parts <= 8:
        for pair in range(parts // 2):
            body(pair)
    else:

        @pl.loop(0, parts // 2)
        def _(pair):
            body(pair)


class Sweeper:
    def __init__(self, parts, faces, gather, listing, aux, outs, work):
        self.parts, self.faces = parts, faces
        self.gather, self.listing, self.aux = gather, listing, aux
        self.outs, self.work = outs, work

    def clear_rim(self):
        zero = jnp.zeros((ROWS, LANES), BF)
        self.outs[0] = zero
        self.outs[self.parts + 1] = zero

    def set_drive(self, state, decay_row, forcing=None):
        def body(pair):
            for side in range(2):
                part = 2 * pair + side
                drive = state[part].astype(F32) * self.aux[part, decay_row : decay_row + 1, :]
                if forcing is not None:
                    drive = drive + forcing(part).astype(F32)
                self.work[
                    pair, self.faces * ROWS :, side * LANES : (side + 1) * LANES
                ] = drive.astype(BF)

        over_pairs(self.parts, body)

    def sweep(self, source, target, table, extra=None):
        lane = lax.broadcasted_iota(jnp.int32, (ROWS, LANES), 1)

        def listed(pair):
            both = jnp.concatenate([source[2 * pair], source[2 * pair + 1]], axis=1)
            chosen = dot(both, self.listing[pair]).astype(BF)
            self.outs[2 * pair + 1] = chosen[:, :LANES]
            self.outs[2 * pair + 2] = chosen[:, LANES:]

        def gathered(pair):
            for side in range(2):
                part = 2 * pair + side
                rim = jnp.where(lane < LANES // 2, self.outs[part], self.outs[part + 2])
                extended = jnp.concatenate([source[part], rim], axis=1)
                found = dot(extended, self.gather[part]).astype(BF)
                for face in range(self.faces):
                    self.work[
                        pair,
                        face * ROWS : (face + 1) * ROWS,
                        side * LANES : (side + 1) * LANES,
                    ] = found[:, face * LANES : (face + 1) * LANES]

        def applied(pair):
            both = dot(table[...], self.work[pair])
            for side in range(2):
                part = 2 * pair + side
                result = both[:, side * LANES : (side + 1) * LANES]
                prism = jnp.concatenate(
                    [result[ROWS:], jnp.zeros((ROWS - PROWS, LANES), F32)], axis=0
                )
                kind = self.aux[part, 0:1, :]
                value = jnp.where(kind == 0.0, result[:ROWS], prism)
                if extra is not None:
                    value = value + extra[part].astype(F32)
                target[part] = value.astype(BF)

        over_pairs(self.parts, listed)
        over_pairs(self.parts, gathered)
        over_pairs(self.parts, applied)

    def step(self, state, other, table, decay_row, forcing=None, extra=None):
        self.set_drive(state, decay_row, forcing)
        places = [state, other]
        for turn in range(SWEEPS):
            last = turn + 1 == SWEEPS
            self.sweep(
                places[turn % 2], places[(turn + 1) % 2], table, extra if last else None
            )


def pack_kernel(space, intervals, forcing, initial, damping, etype, send_index, conn, *messages):
    place = Place(space, intervals)
    width = initial.shape[0]
    faces = conn.shape[0]
    lists = pltpu.roll(jnp.broadcast_to(send_index[...].astype(F32), (8, LANES)), LANES // 2, 1)
    kinds = jnp.broadcast_to(etype[0].astype(F32), (1, LANES))
    first = jnp.concatenate([conn[...].astype(F32), kinds, lists[:1]], axis=0).astype(BF)
    rest = damping[...]
    pieces = []
    for _ in range(3):
        pieces.append(rest.astype(BF))
        rest = rest - pieces[-1].astype(F32)
    second = jnp.concatenate(pieces, axis=0)
    for turn in range(intervals):
        interval = lax.rem(place.next_interval + turn, intervals)
        out = messages[turn]
        for index in range(COARSEN):
            out[index, :width] = forcing[interval * COARSEN + index]
        out[COARSEN, :width] = initial[...]
        out[0, width : width + faces + 2] = first
        out[1, width : width + 3] = second


def fine_kernel(space, intervals, width, faces, *refs):
    messages = refs[:space]
    table, residual, gather, listing, aux, forcing, start = refs[space : space + 7]
    other, outs, work = refs[space + 7 :]
    place = Place(space, intervals)

    @pl.when(place.active)
    def _():
        sweeper = Sweeper(space, faces, gather, listing, aux, outs, work)
        sweeper.clear_rim()
        rows = lax.broadcasted_iota(jnp.int32, (ROWS, LANES), 0).astype(F32)
        full = lax.broadcasted_iota(jnp.int32, (2 * LANES, LANES), 0).astype(F32)
        half = full[:LANES]
        zero = jnp.zeros((LANES, LANES), BF)
        for turn in range(space):
            part = lax.rem(place.position - turn + space, space)
            message = messages[turn]
            for index in range(COARSEN):
                forcing[part, index] = message[index]
            first = message[0, width : width + faces + 2].astype(F32)
            second = message[1, width : width + 3].astype(F32)
            kind = first[faces : faces + 1]
            damping = (second[0:1] + second[1:2]) + second[2:3]
            aux[part] = jnp.concatenate(
                [
                    kind,
                    jnp.exp(-damping),
                    jnp.exp(-COARSEN * damping),
                    jnp.zeros((5, LANES), F32),
                ],
                axis=0,
            )
            for face in range(faces):
                found = full == first[face : face + 1]
                if face == faces - 1:
                    found = found & (kind == 0.0)
                gather[part, :, face * LANES : (face + 1) * LANES] = jnp.where(
                    found, 1.0, 0.0
                ).astype(BF)
            picks = jnp.where(half == first[faces + 1 : faces + 2], 1.0, 0.0).astype(BF)
            odd = lax.rem(part, 2) == 1
            left = jnp.where(odd, 0.0, 1.0).astype(BF)
            right = jnp.where(odd, 1.0, 0.0).astype(BF)
            listing[part // 2, pl.ds(pl.multiple_of(lax.rem(part, 2) * LANES, LANES), LANES), :] = (
                jnp.concatenate([picks * left, picks * right], axis=1)
            )
            limit = jnp.where(kind == 0.0, float(width), float(PRISM))
            wanted = (rows < limit) & (place.number == 0)
            start[part] = jnp.where(wanted, message[COARSEN].astype(F32), 0.0).astype(BF)

        residual[...] = start[...]

        @pl.loop(0, COARSEN)
        def _(index):
            sweeper.step(residual, other, table, 1, lambda part: forcing[part, index])


def advance(sweeper, state, other, table, powers, extra=None):
    if powers > 1:

        @pl.loop(0, powers - 1)
        def _(turn):
            sweeper.step(state, other, table, 2)

    sweeper.step(state, other, table, 2, extra=extra)


def near_kernel(space, intervals, faces, *refs):
    terms = refs[:intervals]
    table, gather, listing, aux, result, other, outs, work = refs[intervals:]
    place = Place(space, intervals)

    @pl.when(place.active)
    def _():
        sweeper = Sweeper(space, faces, gather, listing, aux, outs, work)
        sweeper.clear_rim()
        result[...] = terms[0][...]
        for term in terms[1:]:
            advance(sweeper, result, other, table, 1, term)


def far_kernel(space, intervals, faces, *refs):
    *terms, table, gather, listing, aux, result, other, outs, work = refs
    place = Place(space, intervals)

    @pl.when(place.active)
    def _():
        sweeper = Sweeper(space, faces, gather, listing, aux, outs, work)
        sweeper.clear_rim()
        result[...] = sum_of(terms)
        advance(sweeper, result, other, table, intervals)


def sum_of(terms):
    total = terms[0][...]
    for term in terms[1:]:
        total = (total.astype(F32) + term[...].astype(F32)).astype(BF)
    return total


def final_kernel(space, intervals, width, faces, *refs):
    earlier, inner, partial, residual, start, forcing = refs[:6]
    fine_table, coarse_table, gather, listing, aux = refs[6:11]
    pieces = refs[11 : 11 + space]
    before, states, other, outs, work = refs[11 + space :]
    place = Place(space, intervals)

    @pl.when(place.active)
    def _():
        sweeper = Sweeper(space, faces, gather, listing, aux, outs, work)
        sweeper.clear_rim()
        before[...] = sum_of([earlier, inner])
        advance(sweeper, before, other, coarse_table, intervals, partial)
        last = COARSEN - 1
        state = states.at[last]
        state[...] = before[...]
        sweeper.step(state, other, coarse_table, 2, extra=residual)
        first = place.number == 0
        states[0] = jnp.where(first, start[...], before[...])

        @pl.loop(0, last)
        def _(index):
            now = states.at[index]
            sweeper.step(now, other, fine_table, 1, lambda part: forcing[part, index])

            @pl.when(index + 1 < last)
            def _():
                states[index + 1] = now[...]

        for turn in range(space):
            part = lax.rem(place.position + turn, space)
            for index in range(COARSEN):
                pieces[turn][index] = states[index, part][:width]


def gather_kernel(space, intervals, *refs):
    pieces = refs[:space]
    out, sem = refs[space:]
    stride = space // intervals
    place = Place(space, intervals)
    offset = lax.rem(lax.rem(place.window, 2), stride)
    for interval in range(intervals):
        wanted = lax.rem(place.position - offset - interval * stride + 2 * space, space)
        for turn in range(space):

            @pl.when(wanted == turn)
            def _():
                pltpu.make_async_copy(
                    pieces[turn], out.at[pl.ds(interval * COARSEN, COARSEN)], sem.at[interval]
                ).start()

    for interval in range(intervals):
        pltpu.make_async_copy(
            pieces[0], out.at[pl.ds(interval * COARSEN, COARSEN)], sem.at[interval]
        ).wait()


def fold_kernel(fine, coarse, coupling, fine_table, coarse_table, wide):
    faces, width, _ = coupling.shape
    wide[...] = jnp.zeros(wide.shape, F32)
    for face in range(faces):
        wide[:width, face * ROWS : face * ROWS + width] = -coupling[face].astype(F32)
    rows = lax.broadcasted_iota(jnp.int32, (width, width), 0)
    columns = lax.broadcasted_iota(jnp.int32, (width, width), 1)
    wide[:width, faces * ROWS : faces * ROWS + width] = jnp.where(rows == columns, 1.0, 0.0)
    factors = wide[:width].astype(BF)
    for inverse, table in ((fine, fine_table), (coarse, coarse_table)):
        table[...] = jnp.zeros(table.shape, BF)
        table[:width] = dot(inverse[0], factors).astype(BF)
        table[ROWS : ROWS + PRISM] = dot(inverse[1], factors)[:PRISM].astype(BF)


def shards(initial, forcing, damping, block_inv, coarse_inv, coupling, etype, send_index, conn):
    width, elems = initial.shape
    faces = conn.shape[0]
    steps = forcing.shape[0]
    intervals = steps // COARSEN
    space = lax.axis_size("space")
    windows = lax.axis_size("tm")
    stride = space // intervals
    params = pltpu.CompilerParams(vmem_limit_bytes=min(56, 2 * space) * MIB)
    state_shape = jax.ShapeDtypeStruct((space, ROWS, LANES), BF)

    message_shape = jax.ShapeDtypeStruct((COARSEN + 1, ROWS, LANES), BF)
    messages = pl.pallas_call(
        functools.partial(pack_kernel, space, intervals),
        out_shape=[message_shape] * intervals,
        in_specs=[VMEM] * 3 + [pl.BlockSpec(memory_space=pltpu.SMEM)] + [VMEM] * 2,
        out_specs=[VMEM] * intervals,
        compiler_params=params,
        name="pack",
    )(forcing, initial, damping[None], etype, send_index[None], conn)

    received = [messages[0]]
    for turn in range(1, space):
        pairs = []
        for window in range(windows):
            for interval in range(intervals):
                host = host_of(window, interval, space, intervals)
                source = (host - turn) % space
                pairs.append((window * space + source, window * space + host))
        received.append(lax.ppermute(messages[turn // stride], ("tm", "space"), pairs))

    table_shape = jax.ShapeDtypeStruct((ROWS + PROWS, (faces + 1) * ROWS), BF)
    fine_table, coarse_table = pl.pallas_call(
        fold_kernel,
        out_shape=[table_shape] * 2,
        in_specs=[VMEM] * 3,
        out_specs=[VMEM] * 2,
        scratch_shapes=[pltpu.VMEM((ROWS, (faces + 1) * ROWS), F32)],
        compiler_params=params,
        name="fold",
    )(block_inv, coarse_inv, coupling)

    gather_shape = jax.ShapeDtypeStruct((space, 2 * LANES, faces * LANES), BF)
    listing_shape = jax.ShapeDtypeStruct((space // 2, 2 * LANES, 2 * LANES), BF)
    aux_shape = jax.ShapeDtypeStruct((space, 8, LANES), F32)
    forcing_shape = jax.ShapeDtypeStruct((space, COARSEN, ROWS, LANES), BF)
    scratch = [
        pltpu.VMEM((space, ROWS, LANES), BF),
        pltpu.VMEM((space + 2, ROWS, LANES), BF),
        pltpu.VMEM((space // 2, (faces + 1) * ROWS, 2 * LANES), BF),
    ]
    residual, gather, listing, aux, whole_forcing, start = pl.pallas_call(
        functools.partial(fine_kernel, space, intervals, width, faces),
        out_shape=[state_shape, gather_shape, listing_shape, aux_shape, forcing_shape, state_shape],
        in_specs=[VMEM] * (space + 1),
        out_specs=[VMEM] * 6,
        scratch_shapes=scratch,
        compiler_params=params,
        name="fine",
    )(*received, fine_table)

    def from_earlier(value, by):
        pairs = []
        for number in range(by, windows * intervals):
            target = number // intervals
            source = (number - by) // intervals
            pairs.append(
                (
                    source * space + host_of(source, (number - by) % intervals, space, intervals),
                    target * space + host_of(target, number % intervals, space, intervals),
                )
            )
        return lax.ppermute(value, ("tm", "space"), pairs)

    def chain(kernel, terms, name):
        return pl.pallas_call(
            functools.partial(kernel, space, intervals, faces),
            out_shape=state_shape,
            in_specs=[VMEM] * (len(terms) + 4),
            out_specs=VMEM,
            scratch_shapes=scratch,
            compiler_params=params,
            name=name,
        )(*terms, coarse_table, gather, listing, aux)

    near = [from_earlier(residual, by) for by in range(intervals, 0, -1)]
    partial = chain(near_kernel, near, "near")
    earlier, *inner = [
        from_earlier(partial, by * intervals) for by in range(windows - 1, 0, -1)
    ]
    earlier = chain(far_kernel, [earlier], "far")
    for term in inner[:-1]:
        earlier = chain(far_kernel, [earlier, term], "far")

    piece_shape = jax.ShapeDtypeStruct((COARSEN, width, LANES), BF)
    pieces = pl.pallas_call(
        functools.partial(final_kernel, space, intervals, width, faces),
        out_shape=[piece_shape] * space,
        in_specs=[VMEM] * 11,
        out_specs=[VMEM] * space,
        scratch_shapes=[
            pltpu.VMEM((space, ROWS, LANES), BF),
            pltpu.VMEM((COARSEN, space, ROWS, LANES), BF),
        ]
        + scratch,
        compiler_params=params,
        name="final",
    )(
        earlier,
        inner[-1],
        partial,
        residual,
        start,
        whole_forcing,
        fine_table,
        coarse_table,
        gather,
        listing,
        aux,
    )

    returned = [pieces[0]]
    for turn in range(1, space):
        pairs = []
        for window in range(windows):
            for interval in range(intervals):
                host = host_of(window, interval, space, intervals)
                pairs.append((window * space + host, window * space + (host + turn) % space))
        returned.append(lax.ppermute(pieces[turn], ("tm", "space"), pairs))

    return pl.pallas_call(
        functools.partial(gather_kernel, space, intervals),
        out_shape=jax.ShapeDtypeStruct(forcing.shape, BF),
        in_specs=[pl.BlockSpec(memory_space=pl.ANY)] * space,
        out_specs=VMEM,
        scratch_shapes=[pltpu.SemaphoreType.DMA((intervals,))],
        compiler_params=params,
        name="place",
    )(*returned)


def solution(mesh):
    in_specs = (
        P(None, "space"),
        P("tm", None, "space"),
        P("space"),
        P(),
        P(),
        P(),
        P("space"),
        P("space"),
        P(None, "space"),
    )
    out_specs = P("tm", None, "space")
    return jax.shard_map(shards, mesh=mesh, in_specs=in_specs, out_specs=out_specs, check_vma=False)
```

```python
import functools

import jax
import jax.numpy as jnp
from jax import lax
from jax.experimental import pallas as pl
from jax.experimental.pallas import tpu as pltpu
from jax.sharding import PartitionSpec as P

PRISM = 90
SWEEPS = 2
COARSEN = 4
ROWS = 144
PROWS = 96
LANES = 128
PICKED = 2
BF = jnp.bfloat16
F32 = jnp.float32
VMEM = pl.BlockSpec(memory_space=pltpu.VMEM)
MIB = 1024 * 1024


def dot(a, b):
    return jnp.dot(a, b, preferred_element_type=F32)


def host_of(window, interval, space, intervals):
    stride = space // intervals
    return (interval * stride + (window % 2) % stride) % space


def away(host, turn, window, space):
    return (host + (turn if window % 2 == 0 else -turn)) % space


class Place:
    def __init__(self, space, intervals):
        stride = space // intervals
        self.window = lax.axis_index("tm")
        self.space = space
        self.sign = 1 - 2 * lax.rem(self.window, 2)
        self.position = lax.axis_index("space")
        shifted = lax.rem(
            self.position - lax.rem(lax.rem(self.window, 2), stride) + space, space
        )
        self.active = lax.rem(shifted, stride) == 0
        self.interval = shifted // stride
        below = shifted // stride
        above = lax.rem((shifted + stride - 1) // stride, intervals)
        self.nearest = jnp.where(self.sign > 0, below, above)
        self.number = self.window * intervals + self.interval


    def away(self, turn):
        return lax.rem(self.position + self.sign * turn + self.space, self.space)


def over_pairs(parts, body):
    if parts <= 8:
        for pair in range(parts // 2):
            body(pair)
    else:

        @pl.loop(0, parts // 2)
        def _(pair):
            body(pair)


class Sweeper:
    def __init__(self, parts, faces, gather, listing, aux, outs, work):
        self.parts, self.faces = parts, faces
        self.gather, self.listing, self.aux = gather, listing, aux
        self.outs, self.work = outs, work

    def clear_rim(self):
        zero = jnp.zeros((ROWS, LANES), BF)
        self.outs[0] = zero
        self.outs[self.parts + 1] = zero

    def set_drive(self, state, decay_row, forcing=None):
        def body(pair):
            for side in range(2):
                part = 2 * pair + side
                drive = state[part].astype(F32) * self.aux[part, decay_row : decay_row + 1, :]
                if forcing is not None:
                    drive = drive + forcing(part).astype(F32)
                self.work[
                    pair, self.faces * ROWS :, side * LANES : (side + 1) * LANES
                ] = drive.astype(BF)

        over_pairs(self.parts, body)

    def sweep(self, source, target, table, extra=None):
        lane = lax.broadcasted_iota(jnp.int32, (ROWS, LANES), 1)

        def listed(pair):
            both = jnp.concatenate([source[2 * pair], source[2 * pair + 1]], axis=1)
            chosen = dot(both, self.listing[pair]).astype(BF)
            self.outs[2 * pair + 1] = chosen[:, :LANES]
            self.outs[2 * pair + 2] = chosen[:, LANES:]

        def gathered(pair):
            for side in range(2):
                part = 2 * pair + side
                rim = jnp.where(lane < LANES // 2, self.outs[part], self.outs[part + 2])
                own = source[part]
                found = dot(jnp.concatenate([own, rim], axis=1), self.gather[part]).astype(BF)
                own, rim = own.astype(F32), rim.astype(F32)
                for face in range(self.faces):
                    if face < self.faces - PICKED:
                        value = found[:, face * LANES : (face + 1) * LANES]
                    else:
                        row = 3 + face - (self.faces - PICKED)
                        place = jnp.broadcast_to(
                            self.aux[part, row : row + 1, :].astype(jnp.int32), (ROWS, LANES)
                        )
                        lanes = place & (LANES - 1)
                        inner = jnp.where(place < 0, 0.0, jnp.take_along_axis(own, lanes, axis=1))
                        outer = jnp.take_along_axis(rim, lanes, axis=1)
                        value = jnp.where(place < LANES, inner, outer).astype(BF)
                    self.work[
                        pair,
                        face * ROWS : (face + 1) * ROWS,
                        side * LANES : (side + 1) * LANES,
                    ] = value

        def applied(pair):
            both = dot(table[...], self.work[pair])
            for side in range(2):
                part = 2 * pair + side
                result = both[:, side * LANES : (side + 1) * LANES]
                prism = jnp.concatenate(
                    [result[ROWS:], jnp.zeros((ROWS - PROWS, LANES), F32)], axis=0
                )
                kind = self.aux[part, 0:1, :]
                value = jnp.where(kind == 0.0, result[:ROWS], prism)
                if extra is not None:
                    value = value + extra[part].astype(F32)
                target[part] = value.astype(BF)

        over_pairs(self.parts, listed)
        over_pairs(self.parts, gathered)
        over_pairs(self.parts, applied)

    def step(self, state, other, table, decay_row, forcing=None, extra=None):
        self.set_drive(state, decay_row, forcing)
        places = [state, other]
        for turn in range(SWEEPS):
            last = turn + 1 == SWEEPS
            self.sweep(
                places[turn % 2], places[(turn + 1) % 2], table, extra if last else None
            )


def pack_kernel(space, intervals, etype, *refs):
    sources, refs = refs[:5], refs[5:]
    messages, refs = refs[:intervals], refs[intervals:]
    held, (packed, in_sem, out_sem) = refs[:5], refs[5:]
    arriving = []
    for index in range(5):
        arriving.append(pltpu.make_async_copy(sources[index], held[index], in_sem.at[index]))
        arriving[-1].start()
    for copy in arriving:
        copy.wait()
    forcing, initial, damping, send_index, conn = held
    place = Place(space, intervals)
    width = initial.shape[0]
    faces = conn.shape[0]
    lists = pltpu.roll(jnp.broadcast_to(send_index[...].astype(F32), (8, LANES)), LANES // 2, 1)
    kinds = jnp.broadcast_to(etype[0].astype(F32), (1, LANES))
    first = jnp.concatenate([conn[...].astype(F32), kinds, lists[:1]], axis=0).astype(BF)
    rest = damping[...]
    pieces = []
    for _ in range(3):
        pieces.append(rest.astype(BF))
        rest = rest - pieces[-1].astype(F32)
    second = jnp.concatenate(pieces, axis=0)
    leaving = []
    for turn in range(intervals):
        interval = lax.rem(place.nearest - place.sign * turn + intervals, intervals)
        out = packed.at[turn]
        for index in range(COARSEN):
            out[index, :width] = forcing[interval * COARSEN + index]
        out[COARSEN, :width] = initial[...]
        out[0, width : width + faces + 2] = first
        out[1, width : width + 3] = second
        leaving.append(pltpu.make_async_copy(out, messages[turn], out_sem.at[turn]))
        leaving[-1].start()
    for copy in leaving:
        copy.wait()


def fine_kernel(space, intervals, width, faces, *refs):
    messages = refs[:space]
    table, residual, gather, listing, aux, forcing, start = refs[space : space + 7]
    other, outs, work = refs[space + 7 :]
    place = Place(space, intervals)

    @pl.when(place.active)
    def _():
        sweeper = Sweeper(space, faces, gather, listing, aux, outs, work)
        sweeper.clear_rim()
        rows = lax.broadcasted_iota(jnp.int32, (ROWS, LANES), 0).astype(F32)
        full = lax.broadcasted_iota(jnp.int32, (2 * LANES, LANES), 0).astype(F32)
        half = full[:LANES]
        zero = jnp.zeros((LANES, LANES), BF)
        for turn in range(space):
            part = place.away(turn)
            message = messages[turn]
            for index in range(COARSEN):
                forcing[part, index] = message[index]
            first = message[0, width : width + faces + 2].astype(F32)
            second = message[1, width : width + 3].astype(F32)
            kind = first[faces : faces + 1]
            damping = (second[0:1] + second[1:2]) + second[2:3]
            picked = [first[face : face + 1] for face in range(faces - PICKED, faces)]
            picked[-1] = jnp.where(kind == 0.0, picked[-1], -1.0)
            aux[part] = jnp.concatenate(
                [
                    kind,
                    jnp.exp(-damping),
                    jnp.exp(-COARSEN * damping),
                    *picked,
                    jnp.zeros((5 - PICKED, LANES), F32),
                ],
                axis=0,
            )
            for face in range(faces - PICKED):
                found = full == first[face : face + 1]
                gather[part, :, face * LANES : (face + 1) * LANES] = jnp.where(
                    found, 1.0, 0.0
                ).astype(BF)
            picks = jnp.where(half == first[faces + 1 : faces + 2], 1.0, 0.0).astype(BF)
            odd = lax.rem(part, 2) == 1
            left = jnp.where(odd, 0.0, 1.0).astype(BF)
            right = jnp.where(odd, 1.0, 0.0).astype(BF)
            listing[part // 2, pl.ds(pl.multiple_of(lax.rem(part, 2) * LANES, LANES), LANES), :] = (
                jnp.concatenate([picks * left, picks * right], axis=1)
            )
            limit = jnp.where(kind == 0.0, float(width), float(PRISM))
            wanted = (rows < limit) & (place.number == 0)
            start[part] = jnp.where(wanted, message[COARSEN].astype(F32), 0.0).astype(BF)

        residual[...] = start[...]

        @pl.loop(0, COARSEN)
        def _(index):
            sweeper.step(residual, other, table, 1, lambda part: forcing[part, index])


def added(first, second):
    return (first.astype(F32) + second.astype(F32)).astype(BF)


def horner(sweeper, state, other, table, terms, known):
    for index, term in enumerate(terms):

        @pl.when(known + index >= 0)
        def _():
            sweeper.step(state, other, table, 2, extra=term)

        @pl.when(known + index < 0)
        def _():
            state[...] = term[...]


def near_kernel(space, intervals, windows, faces, *refs):
    terms = refs[:intervals]
    table, gather, listing, aux, result, other, outs, work = refs[intervals:]
    place = Place(space, intervals)

    @pl.when(place.active & (place.window + 1 < windows))
    def _():
        sweeper = Sweeper(space, faces, gather, listing, aux, outs, work)
        sweeper.clear_rim()
        result[...] = terms[0][...]
        horner(sweeper, result, other, table, terms[1:], place.number - intervals)


def far_kernel(space, intervals, least, faces, *refs):
    *terms, table, gather, listing, aux, result, other, outs, work = refs
    place = Place(space, intervals)

    @pl.when(place.active & (place.window >= least))
    def _():
        sweeper = Sweeper(space, faces, gather, listing, aux, outs, work)
        sweeper.clear_rim()
        result[...] = added(terms[0][...], terms[1][...]) if len(terms) > 1 else terms[0][...]

        @pl.loop(0, intervals)
        def _(turn):
            sweeper.step(result, other, table, 2)

    @pl.when(place.window < least)
    def _():
        result[...] = jnp.zeros(result.shape, BF)


def final_kernel(space, intervals, width, faces, *refs):
    near, refs = refs[:intervals], refs[intervals:]
    earlier, inner, residual, start, forcing = refs[:5]
    fine_table, coarse_table, gather, listing, aux = refs[5:10]
    pieces = refs[10 : 10 + space]
    before, states, other, outs, work = refs[10 + space :]
    place = Place(space, intervals)

    @pl.when(place.active)
    def _():
        sweeper = Sweeper(space, faces, gather, listing, aux, outs, work)
        sweeper.clear_rim()
        before[...] = added(earlier[...], inner[...])
        horner(sweeper, before, other, coarse_table, near, place.number - intervals - 1)
        last = COARSEN - 1
        state = states.at[last]
        state[...] = before[...]
        sweeper.step(state, other, coarse_table, 2, extra=residual)
        first = place.number == 0
        states[0] = jnp.where(first, start[...], before[...])

        @pl.loop(0, last)
        def _(index):
            now = states.at[index]
            sweeper.step(now, other, fine_table, 1, lambda part: forcing[part, index])

            @pl.when(index + 1 < last)
            def _():
                states[index + 1] = now[...]

        for turn in range(space):
            part = place.away(turn)
            for index in range(COARSEN):
                pieces[turn][index] = states[index, part][:width]


def gather_kernel(space, intervals, *refs):
    pieces = refs[:space]
    out, sem = refs[space:]
    stride = space // intervals
    place = Place(space, intervals)
    offset = lax.rem(lax.rem(place.window, 2), stride)
    for interval in range(intervals):
        host = interval * stride + offset
        wanted = lax.rem(place.sign * (place.position - host) + 2 * space, space)
        for turn in range(space):

            @pl.when(wanted == turn)
            def _():
                pltpu.make_async_copy(
                    pieces[turn], out.at[pl.ds(interval * COARSEN, COARSEN)], sem.at[interval]
                ).start()

    for interval in range(intervals):
        pltpu.make_async_copy(
            pieces[0], out.at[pl.ds(interval * COARSEN, COARSEN)], sem.at[interval]
        ).wait()


def fold_kernel(fine, coarse, coupling, fine_table, coarse_table, wide):
    faces, width, _ = coupling.shape
    wide[...] = jnp.zeros(wide.shape, F32)
    for face in range(faces):
        wide[:width, face * ROWS : face * ROWS + width] = -coupling[face].astype(F32)
    rows = lax.broadcasted_iota(jnp.int32, (width, width), 0)
    columns = lax.broadcasted_iota(jnp.int32, (width, width), 1)
    wide[:width, faces * ROWS : faces * ROWS + width] = jnp.where(rows == columns, 1.0, 0.0)
    factors = wide[:width].astype(BF)
    for inverse, table in ((fine, fine_table), (coarse, coarse_table)):
        table[...] = jnp.zeros(table.shape, BF)
        table[:width] = dot(inverse[0], factors).astype(BF)
        table[ROWS : ROWS + PRISM] = dot(inverse[1], factors)[:PRISM].astype(BF)


def shards(initial, forcing, damping, block_inv, coarse_inv, coupling, etype, send_index, conn):
    width, elems = initial.shape
    faces = conn.shape[0]
    steps = forcing.shape[0]
    intervals = steps // COARSEN
    space = lax.axis_size("space")
    windows = lax.axis_size("tm")
    stride = space // intervals
    params = pltpu.CompilerParams(vmem_limit_bytes=min(56, 2 * space) * MIB)
    state_shape = jax.ShapeDtypeStruct((space, ROWS, LANES), BF)

    hbm = pl.BlockSpec(memory_space=pltpu.HBM)
    packing = [forcing, initial, damping[None], send_index[None], conn]
    message_shape = jax.ShapeDtypeStruct((COARSEN + 1, ROWS, LANES), BF)
    messages = pl.pallas_call(
        functools.partial(pack_kernel, space, intervals),
        out_shape=[message_shape] * intervals,
        in_specs=[pl.BlockSpec(memory_space=pltpu.SMEM)] + [hbm] * 5,
        out_specs=[hbm] * intervals,
        scratch_shapes=[pltpu.VMEM(array.shape, array.dtype) for array in packing]
        + [
            pltpu.VMEM((intervals, COARSEN + 1, ROWS, LANES), BF),
            pltpu.SemaphoreType.DMA((5,)),
            pltpu.SemaphoreType.DMA((intervals,)),
        ],
        compiler_params=pltpu.CompilerParams(vmem_limit_bytes=60 * MIB),
        name="pack",
    )(etype, *packing)

    received = [messages[0]] * space
    turns = sorted(range(1, space), key=lambda turn: turn % stride == 0)
    for turn in turns:
        pairs = []
        for window in range(windows):
            for interval in range(intervals):
                host = host_of(window, interval, space, intervals)
                source = away(host, turn, window, space)
                pairs.append((window * space + source, window * space + host))
        received[turn] = lax.ppermute(messages[turn // stride], ("tm", "space"), pairs)

    table_shape = jax.ShapeDtypeStruct((ROWS + PROWS, (faces + 1) * ROWS), BF)
    fine_table, coarse_table = pl.pallas_call(
        fold_kernel,
        out_shape=[table_shape] * 2,
        in_specs=[VMEM] * 3,
        out_specs=[VMEM] * 2,
        scratch_shapes=[pltpu.VMEM((ROWS, (faces + 1) * ROWS), F32)],
        compiler_params=params,
        name="fold",
    )(block_inv, coarse_inv, coupling)

    gather_shape = jax.ShapeDtypeStruct((space, 2 * LANES, (faces - PICKED) * LANES), BF)
    listing_shape = jax.ShapeDtypeStruct((space // 2, 2 * LANES, 2 * LANES), BF)
    aux_shape = jax.ShapeDtypeStruct((space, 8, LANES), F32)
    forcing_shape = jax.ShapeDtypeStruct((space, COARSEN, ROWS, LANES), BF)
    scratch = [
        pltpu.VMEM((space, ROWS, LANES), BF),
        pltpu.VMEM((space + 2, ROWS, LANES), BF),
        pltpu.VMEM((space // 2, (faces + 1) * ROWS, 2 * LANES), BF),
    ]
    residual, gather, listing, aux, whole_forcing, start = pl.pallas_call(
        functools.partial(fine_kernel, space, intervals, width, faces),
        out_shape=[state_shape, gather_shape, listing_shape, aux_shape, forcing_shape, state_shape],
        in_specs=[VMEM] * (space + 1),
        out_specs=[VMEM] * 6,
        scratch_shapes=scratch,
        compiler_params=params,
        name="fine",
    )(*received, fine_table)

    def from_earlier(value, by):
        pairs = []
        for number in range(by, windows * intervals):
            target = number // intervals
            source = (number - by) // intervals
            pairs.append(
                (
                    source * space + host_of(source, (number - by) % intervals, space, intervals),
                    target * space + host_of(target, number % intervals, space, intervals),
                )
            )
        return lax.ppermute(value, ("tm", "space"), pairs)

    def chain(kernel, number, terms, name):
        return pl.pallas_call(
            functools.partial(kernel, space, intervals, number, faces),
            out_shape=state_shape,
            in_specs=[VMEM] * (len(terms) + 4),
            out_specs=VMEM,
            scratch_shapes=scratch,
            compiler_params=params,
            name=name,
        )(*terms, coarse_table, gather, listing, aux)

    near = [from_earlier(residual, by) for by in range(intervals, 0, -1)]
    partial = chain(near_kernel, windows, near, "near")
    earlier, *inner = [
        from_earlier(partial, by * intervals) for by in range(windows - 1, 0, -1)
    ]
    earlier = chain(far_kernel, windows - 1, [earlier], "far")
    for index, term in enumerate(inner[:-1]):
        earlier = chain(far_kernel, windows - 2 - index, [earlier, term], "far")

    piece_shape = jax.ShapeDtypeStruct((COARSEN, width, LANES), BF)
    pieces = pl.pallas_call(
        functools.partial(final_kernel, space, intervals, width, faces),
        out_shape=[piece_shape] * space,
        in_specs=[VMEM] * (intervals + 10),
        out_specs=[VMEM] * space,
        scratch_shapes=[
            pltpu.VMEM((space, ROWS, LANES), BF),
            pltpu.VMEM((COARSEN, space, ROWS, LANES), BF),
        ]
        + scratch,
        compiler_params=params,
        name="final",
    )(
        *near,
        earlier,
        inner[-1],
        residual,
        start,
        whole_forcing,
        fine_table,
        coarse_table,
        gather,
        listing,
        aux,
    )

    returned = [pieces[0]] * space
    for turn in turns:
        pairs = []
        for window in range(windows):
            for interval in range(intervals):
                host = host_of(window, interval, space, intervals)
                target = away(host, turn, window, space)
                pairs.append((window * space + host, window * space + target))
        returned[turn] = lax.ppermute(pieces[turn], ("tm", "space"), pairs)

    return pl.pallas_call(
        functools.partial(gather_kernel, space, intervals),
        out_shape=jax.ShapeDtypeStruct(forcing.shape, BF),
        in_specs=[pl.BlockSpec(memory_space=pl.ANY)] * space,
        out_specs=VMEM,
        scratch_shapes=[pltpu.SemaphoreType.DMA((intervals,))],
        compiler_params=params,
        name="place",
    )(*returned)


def solution(mesh):
    in_specs = (
        P(None, "space"),
        P("tm", None, "space"),
        P("space"),
        P(),
        P(),
        P(),
        P("space"),
        P("space"),
        P(None, "space"),
    )
    out_specs = P("tm", None, "space")
    return jax.shard_map(shards, mesh=mesh, in_specs=in_specs, out_specs=out_specs, check_vma=False)
```

```python
import functools

import jax
import jax.numpy as jnp
from jax import lax
from jax.experimental import pallas as pl
from jax.experimental.pallas import tpu as pltpu
from jax.sharding import PartitionSpec as P

PRISM = 90
SWEEPS = 2
COARSEN = 4
ROWS = 144
PROWS = 96
LANES = 128
PICKED = 2
BF = jnp.bfloat16
F32 = jnp.float32
VMEM = pl.BlockSpec(memory_space=pltpu.VMEM)
MIB = 1024 * 1024


def dot(a, b):
    return jnp.dot(a, b, preferred_element_type=F32)


def rank_of(interval, intervals):
    return (interval % 2) * (intervals // 2) + interval // 2


def interval_at(rank, intervals):
    half = intervals // 2
    return lax.rem(rank, half) * 2 + rank // half


def host_of(window, interval, space, intervals):
    stride = space // intervals
    return (rank_of(interval, intervals) * stride + (window % 2) % stride) % space


def away(host, turn, window, space):
    return (host + (turn if window % 2 == 0 else -turn)) % space


class Place:
    def __init__(self, space, intervals):
        stride = space // intervals
        self.window = lax.axis_index("tm")
        self.space = space
        self.sign = 1 - 2 * lax.rem(self.window, 2)
        self.position = lax.axis_index("space")
        shifted = lax.rem(
            self.position - lax.rem(lax.rem(self.window, 2), stride) + space, space
        )
        self.active = lax.rem(shifted, stride) == 0
        self.interval = interval_at(shifted // stride, intervals)
        below = shifted // stride
        above = lax.rem((shifted + stride - 1) // stride, intervals)
        self.nearest = jnp.where(self.sign > 0, below, above)
        self.number = self.window * intervals + self.interval


    def away(self, turn):
        return lax.rem(self.position + self.sign * turn + self.space, self.space)


def over_pairs(parts, body):
    if parts <= 8:
        for pair in range(parts // 2):
            body(pair)
    else:

        @pl.loop(0, parts // 2)
        def _(pair):
            body(pair)


class Sweeper:
    def __init__(self, parts, faces, gather, listing, aux, outs, work):
        self.parts, self.faces = parts, faces
        self.gather, self.listing, self.aux = gather, listing, aux
        self.outs, self.work = outs, work

    def clear_rim(self):
        zero = jnp.zeros((ROWS, LANES), BF)
        self.outs[0] = zero
        self.outs[self.parts + 1] = zero

    def set_drive(self, state, decay_row, forcing=None):
        def body(pair):
            for side in range(2):
                part = 2 * pair + side
                drive = state[part].astype(F32) * self.aux[part, decay_row : decay_row + 1, :]
                if forcing is not None:
                    drive = drive + forcing(part).astype(F32)
                self.work[
                    pair, self.faces * ROWS :, side * LANES : (side + 1) * LANES
                ] = drive.astype(BF)

        over_pairs(self.parts, body)

    def sweep(self, source, target, table, extra=None):
        lane = lax.broadcasted_iota(jnp.int32, (ROWS, LANES), 1)

        def listed(pair):
            both = jnp.concatenate([source[2 * pair], source[2 * pair + 1]], axis=1)
            chosen = dot(both, self.listing[pair]).astype(BF)
            self.outs[2 * pair + 1] = chosen[:, :LANES]
            self.outs[2 * pair + 2] = chosen[:, LANES:]

        def gathered(pair):
            for side in range(2):
                part = 2 * pair + side
                rim = jnp.where(lane < LANES // 2, self.outs[part], self.outs[part + 2])
                own = source[part]
                found = dot(jnp.concatenate([own, rim], axis=1), self.gather[part]).astype(BF)
                own, rim = own.astype(F32), rim.astype(F32)
                for face in range(self.faces):
                    if face < self.faces - PICKED:
                        value = found[:, face * LANES : (face + 1) * LANES]
                    else:
                        row = 3 + face - (self.faces - PICKED)
                        place = jnp.broadcast_to(
                            self.aux[part, row : row + 1, :].astype(jnp.int32), (ROWS, LANES)
                        )
                        lanes = place & (LANES - 1)
                        inner = jnp.where(place < 0, 0.0, jnp.take_along_axis(own, lanes, axis=1))
                        outer = jnp.take_along_axis(rim, lanes, axis=1)
                        value = jnp.where(place < LANES, inner, outer).astype(BF)
                    self.work[
                        pair,
                        face * ROWS : (face + 1) * ROWS,
                        side * LANES : (side + 1) * LANES,
                    ] = value

        def applied(pair):
            both = dot(table[...], self.work[pair])
            for side in range(2):
                part = 2 * pair + side
                result = both[:, side * LANES : (side + 1) * LANES]
                prism = jnp.concatenate(
                    [result[ROWS:], jnp.zeros((ROWS - PROWS, LANES), F32)], axis=0
                )
                kind = self.aux[part, 0:1, :]
                value = jnp.where(kind == 0.0, result[:ROWS], prism)
                if extra is not None:
                    value = value + extra[part].astype(F32)
                target[part] = value.astype(BF)

        over_pairs(self.parts, listed)
        over_pairs(self.parts, gathered)
        over_pairs(self.parts, applied)

    def step(self, state, other, table, decay_row, forcing=None, extra=None):
        self.set_drive(state, decay_row, forcing)
        places = [state, other]
        for turn in range(SWEEPS):
            last = turn + 1 == SWEEPS
            self.sweep(
                places[turn % 2], places[(turn + 1) % 2], table, extra if last else None
            )


def pack_kernel(space, intervals, etype, *refs):
    sources, refs = refs[:5], refs[5:]
    messages, refs = refs[:intervals], refs[intervals:]
    held, (wide, packed, in_sem, out_sem) = refs[:5], refs[5:]
    arriving = []
    for index in range(5):
        arriving.append(pltpu.make_async_copy(sources[index], held[index], in_sem.at[index]))
        arriving[-1].start()
    for copy in arriving:
        copy.wait()
    forcing, initial, damping, send_index, conn = held
    steps = forcing.shape[1]
    wide[...] = forcing[...].astype(F32).reshape(wide.shape)
    place = Place(space, intervals)
    width = initial.shape[0]
    faces = conn.shape[0]
    lists = pltpu.roll(jnp.broadcast_to(send_index[...].astype(F32), (8, LANES)), LANES // 2, 1)
    kinds = jnp.broadcast_to(etype[0].astype(F32), (1, LANES))
    first = jnp.concatenate([conn[...].astype(F32), kinds, lists[:1]], axis=0).astype(BF)
    rest = damping[...]
    pieces = []
    for _ in range(3):
        pieces.append(rest.astype(BF))
        rest = rest - pieces[-1].astype(F32)
    second = jnp.concatenate(pieces, axis=0)
    leaving = []
    for turn in range(intervals):
        rank = lax.rem(place.nearest - place.sign * turn + intervals, intervals)
        interval = interval_at(rank, intervals)
        out = packed.at[turn]
        for index in range(COARSEN):
            rows = pl.ds(interval * COARSEN + index, width, stride=steps)
            out[index, :width] = wide[rows, :].astype(BF)
        out[COARSEN, :width] = initial[...]
        out[0, width : width + faces + 2] = first
        out[1, width : width + 3] = second
        leaving.append(pltpu.make_async_copy(out, messages[turn], out_sem.at[turn]))
        leaving[-1].start()
    for copy in leaving:
        copy.wait()


def fine_kernel(space, intervals, width, faces, *refs):
    messages = refs[:space]
    table, residual, gather, listing, aux, forcing, start = refs[space : space + 7]
    other, outs, work = refs[space + 7 :]
    place = Place(space, intervals)

    @pl.when(place.active)
    def _():
        sweeper = Sweeper(space, faces, gather, listing, aux, outs, work)
        sweeper.clear_rim()
        rows = lax.broadcasted_iota(jnp.int32, (ROWS, LANES), 0).astype(F32)
        full = lax.broadcasted_iota(jnp.int32, (2 * LANES, LANES), 0).astype(F32)
        half = full[:LANES]
        zero = jnp.zeros((LANES, LANES), BF)
        for turn in range(space):
            part = place.away(turn)
            message = messages[turn]
            for index in range(COARSEN):
                forcing[part, index] = message[index]
            first = message[0, width : width + faces + 2].astype(F32)
            second = message[1, width : width + 3].astype(F32)
            kind = first[faces : faces + 1]
            damping = (second[0:1] + second[1:2]) + second[2:3]
            picked = [first[face : face + 1] for face in range(faces - PICKED, faces)]
            picked[-1] = jnp.where(kind == 0.0, picked[-1], -1.0)
            aux[part] = jnp.concatenate(
                [
                    kind,
                    jnp.exp(-damping),
                    jnp.exp(-COARSEN * damping),
                    *picked,
                    jnp.zeros((5 - PICKED, LANES), F32),
                ],
                axis=0,
            )
            for face in range(faces - PICKED):
                found = full == first[face : face + 1]
                gather[part, :, face * LANES : (face + 1) * LANES] = jnp.where(
                    found, 1.0, 0.0
                ).astype(BF)
            picks = jnp.where(half == first[faces + 1 : faces + 2], 1.0, 0.0).astype(BF)
            odd = lax.rem(part, 2) == 1
            left = jnp.where(odd, 0.0, 1.0).astype(BF)
            right = jnp.where(odd, 1.0, 0.0).astype(BF)
            listing[part // 2, pl.ds(pl.multiple_of(lax.rem(part, 2) * LANES, LANES), LANES), :] = (
                jnp.concatenate([picks * left, picks * right], axis=1)
            )
            limit = jnp.where(kind == 0.0, float(width), float(PRISM))
            wanted = (rows < limit) & (place.number == 0)
            start[part] = jnp.where(wanted, message[COARSEN].astype(F32), 0.0).astype(BF)

        residual[...] = start[...]

        @pl.loop(0, COARSEN)
        def _(index):
            sweeper.step(residual, other, table, 1, lambda part: forcing[part, index])


def added(first, second):
    return (first.astype(F32) + second.astype(F32)).astype(BF)


def horner(sweeper, state, other, table, terms, known):
    for index, term in enumerate(terms):

        @pl.when(known + index >= 0)
        def _():
            sweeper.step(state, other, table, 2, extra=term)

        @pl.when(known + index < 0)
        def _():
            state[...] = term[...]


def near_kernel(space, intervals, windows, faces, *refs):
    terms = refs[:intervals]
    table, gather, listing, aux, result, other, outs, work = refs[intervals:]
    place = Place(space, intervals)

    @pl.when(place.active & (place.window + 1 < windows))
    def _():
        sweeper = Sweeper(space, faces, gather, listing, aux, outs, work)
        sweeper.clear_rim()
        result[...] = terms[0][...]
        horner(sweeper, result, other, table, terms[1:], place.number - intervals)


def far_kernel(space, intervals, least, faces, *refs):
    *terms, table, gather, listing, aux, result, other, outs, work = refs
    place = Place(space, intervals)

    @pl.when(place.active & (place.window >= least))
    def _():
        sweeper = Sweeper(space, faces, gather, listing, aux, outs, work)
        sweeper.clear_rim()
        result[...] = added(terms[0][...], terms[1][...]) if len(terms) > 1 else terms[0][...]

        @pl.loop(0, intervals)
        def _(turn):
            sweeper.step(result, other, table, 2)

    @pl.when(place.window < least)
    def _():
        result[...] = jnp.zeros(result.shape, BF)


def final_kernel(space, intervals, width, faces, *refs):
    near, refs = refs[:intervals], refs[intervals:]
    earlier, inner, residual, start, forcing = refs[:5]
    fine_table, coarse_table, gather, listing, aux = refs[5:10]
    pieces = refs[10 : 10 + space]
    before, states, other, outs, work = refs[10 + space :]
    place = Place(space, intervals)

    @pl.when(place.active)
    def _():
        sweeper = Sweeper(space, faces, gather, listing, aux, outs, work)
        sweeper.clear_rim()
        before[...] = added(earlier[...], inner[...])
        horner(sweeper, before, other, coarse_table, near, place.number - intervals - 1)
        last = COARSEN - 1
        state = states.at[last]
        state[...] = before[...]
        sweeper.step(state, other, coarse_table, 2, extra=residual)
        first = place.number == 0
        states[0] = jnp.where(first, start[...], before[...])

        @pl.loop(0, last)
        def _(index):
            now = states.at[index]
            sweeper.step(now, other, fine_table, 1, lambda part: forcing[part, index])

            @pl.when(index + 1 < last)
            def _():
                states[index + 1] = now[...]

        for turn in range(space):
            part = place.away(turn)
            for index in range(COARSEN):
                pieces[turn][index] = states[index, part][:width]


def gather_kernel(space, intervals, *refs):
    pieces = refs[:space]
    out, sem = refs[space:]
    stride = space // intervals
    place = Place(space, intervals)
    offset = lax.rem(lax.rem(place.window, 2), stride)
    for interval in range(intervals):
        host = rank_of(interval, intervals) * stride + offset
        wanted = lax.rem(place.sign * (place.position - host) + 2 * space, space)
        for turn in range(space):

            @pl.when(wanted == turn)
            def _():
                pltpu.make_async_copy(
                    pieces[turn], out.at[pl.ds(interval * COARSEN, COARSEN)], sem.at[interval]
                ).start()

    for interval in range(intervals):
        pltpu.make_async_copy(
            pieces[0], out.at[pl.ds(interval * COARSEN, COARSEN)], sem.at[interval]
        ).wait()


def fold_kernel(fine, coarse, coupling, fine_table, coarse_table, wide):
    faces, width, _ = coupling.shape
    wide[...] = jnp.zeros(wide.shape, F32)
    for face in range(faces):
        wide[:width, face * ROWS : face * ROWS + width] = -coupling[face].astype(F32)
    rows = lax.broadcasted_iota(jnp.int32, (width, width), 0)
    columns = lax.broadcasted_iota(jnp.int32, (width, width), 1)
    wide[:width, faces * ROWS : faces * ROWS + width] = jnp.where(rows == columns, 1.0, 0.0)
    factors = wide[:width].astype(BF)
    for inverse, table in ((fine, fine_table), (coarse, coarse_table)):
        table[...] = jnp.zeros(table.shape, BF)
        table[:width] = dot(inverse[0], factors).astype(BF)
        table[ROWS : ROWS + PRISM] = dot(inverse[1], factors)[:PRISM].astype(BF)


def shards(initial, forcing, damping, block_inv, coarse_inv, coupling, etype, send_index, conn):
    width, elems = initial.shape
    faces = conn.shape[0]
    steps = forcing.shape[0]
    intervals = steps // COARSEN
    space = lax.axis_size("space")
    windows = lax.axis_size("tm")
    stride = space // intervals
    params = pltpu.CompilerParams(vmem_limit_bytes=min(56, 2 * space) * MIB)
    state_shape = jax.ShapeDtypeStruct((space, ROWS, LANES), BF)

    hbm = pl.BlockSpec(memory_space=pltpu.HBM)
    packing = [jnp.transpose(forcing, (1, 0, 2)), initial, damping[None], send_index[None], conn]
    message_shape = jax.ShapeDtypeStruct((COARSEN + 1, ROWS, LANES), BF)
    messages = pl.pallas_call(
        functools.partial(pack_kernel, space, intervals),
        out_shape=[message_shape] * intervals,
        in_specs=[pl.BlockSpec(memory_space=pltpu.SMEM)] + [hbm] * 5,
        out_specs=[hbm] * intervals,
        scratch_shapes=[pltpu.VMEM(array.shape, array.dtype) for array in packing]
        + [
            pltpu.VMEM((width * steps, LANES), F32),
            pltpu.VMEM((intervals, COARSEN + 1, ROWS, LANES), BF),
            pltpu.SemaphoreType.DMA((5,)),
            pltpu.SemaphoreType.DMA((intervals,)),
        ],
        compiler_params=pltpu.CompilerParams(vmem_limit_bytes=60 * MIB),
        name="pack",
    )(etype, *packing)

    received = [messages[0]] * space
    turns = sorted(range(1, space), key=lambda turn: turn % stride == 0)
    for turn in turns:
        pairs = []
        for window in range(windows):
            for interval in range(intervals):
                host = host_of(window, interval, space, intervals)
                source = away(host, turn, window, space)
                pairs.append((window * space + source, window * space + host))
        received[turn] = lax.ppermute(messages[turn // stride], ("tm", "space"), pairs)

    table_shape = jax.ShapeDtypeStruct((ROWS + PROWS, (faces + 1) * ROWS), BF)
    fine_table, coarse_table = pl.pallas_call(
        fold_kernel,
        out_shape=[table_shape] * 2,
        in_specs=[VMEM] * 3,
        out_specs=[VMEM] * 2,
        scratch_shapes=[pltpu.VMEM((ROWS, (faces + 1) * ROWS), F32)],
        compiler_params=params,
        name="fold",
    )(block_inv, coarse_inv, coupling)

    gather_shape = jax.ShapeDtypeStruct((space, 2 * LANES, (faces - PICKED) * LANES), BF)
    listing_shape = jax.ShapeDtypeStruct((space // 2, 2 * LANES, 2 * LANES), BF)
    aux_shape = jax.ShapeDtypeStruct((space, 8, LANES), F32)
    forcing_shape = jax.ShapeDtypeStruct((space, COARSEN, ROWS, LANES), BF)
    scratch = [
        pltpu.VMEM((space, ROWS, LANES), BF),
        pltpu.VMEM((space + 2, ROWS, LANES), BF),
        pltpu.VMEM((space // 2, (faces + 1) * ROWS, 2 * LANES), BF),
    ]
    residual, gather, listing, aux, whole_forcing, start = pl.pallas_call(
        functools.partial(fine_kernel, space, intervals, width, faces),
        out_shape=[state_shape, gather_shape, listing_shape, aux_shape, forcing_shape, state_shape],
        in_specs=[VMEM] * (space + 1),
        out_specs=[VMEM] * 6,
        scratch_shapes=scratch,
        compiler_params=params,
        name="fine",
    )(*received, fine_table)

    def from_earlier(value, by):
        pairs = []
        for number in range(by, windows * intervals):
            target = number // intervals
            source = (number - by) // intervals
            pairs.append(
                (
                    source * space + host_of(source, (number - by) % intervals, space, intervals),
                    target * space + host_of(target, number % intervals, space, intervals),
                )
            )
        return lax.ppermute(value, ("tm", "space"), pairs)

    def chain(kernel, number, terms, name):
        return pl.pallas_call(
            functools.partial(kernel, space, intervals, number, faces),
            out_shape=state_shape,
            in_specs=[VMEM] * (len(terms) + 4),
            out_specs=VMEM,
            scratch_shapes=scratch,
            compiler_params=params,
            name=name,
        )(*terms, coarse_table, gather, listing, aux)

    near = [from_earlier(residual, by) for by in range(intervals, 0, -1)]
    partial = chain(near_kernel, windows, near, "near")
    earlier, *inner = [
        from_earlier(partial, by * intervals) for by in range(windows - 1, 0, -1)
    ]
    earlier = chain(far_kernel, windows - 1, [earlier], "far")
    for index, term in enumerate(inner[:-1]):
        earlier = chain(far_kernel, windows - 2 - index, [earlier, term], "far")

    piece_shape = jax.ShapeDtypeStruct((COARSEN, width, LANES), BF)
    pieces = pl.pallas_call(
        functools.partial(final_kernel, space, intervals, width, faces),
        out_shape=[piece_shape] * space,
        in_specs=[VMEM] * (intervals + 10),
        out_specs=[VMEM] * space,
        scratch_shapes=[
            pltpu.VMEM((space, ROWS, LANES), BF),
            pltpu.VMEM((COARSEN, space, ROWS, LANES), BF),
        ]
        + scratch,
        compiler_params=params,
        name="final",
    )(
        *near,
        earlier,
        inner[-1],
        residual,
        start,
        whole_forcing,
        fine_table,
        coarse_table,
        gather,
        listing,
        aux,
    )

    returned = [pieces[0]] * space
    for turn in turns:
        pairs = []
        for window in range(windows):
            for interval in range(intervals):
                host = host_of(window, interval, space, intervals)
                target = away(host, turn, window, space)
                pairs.append((window * space + host, window * space + target))
        returned[turn] = lax.ppermute(pieces[turn], ("tm", "space"), pairs)

    return pl.pallas_call(
        functools.partial(gather_kernel, space, intervals),
        out_shape=jax.ShapeDtypeStruct(forcing.shape, BF),
        in_specs=[pl.BlockSpec(memory_space=pl.ANY)] * space,
        out_specs=VMEM,
        scratch_shapes=[pltpu.SemaphoreType.DMA((intervals,))],
        compiler_params=params,
        name="place",
    )(*returned)


def solution(mesh):
    in_specs = (
        P(None, "space"),
        P("tm", None, "space"),
        P("space"),
        P(),
        P(),
        P(),
        P("space"),
        P("space"),
        P(None, "space"),
    )
    out_specs = P("tm", None, "space")
    return jax.shard_map(shards, mesh=mesh, in_specs=in_specs, out_specs=out_specs, check_vma=False)
```

```python
import functools

import jax
import jax.numpy as jnp
from jax import lax
from jax.experimental import pallas as pl
from jax.experimental.pallas import tpu as pltpu
from jax.sharding import PartitionSpec as P

PRISM = 90
SWEEPS = 2
COARSEN = 4
ROWS = 144
PROWS = 96
LANES = 128
PICKED = 2
BF = jnp.bfloat16
F32 = jnp.float32
VMEM = pl.BlockSpec(memory_space=pltpu.VMEM)
MIB = 1024 * 1024


def dot(a, b):
    return jnp.dot(a, b, preferred_element_type=F32)


def rank_of(interval, intervals):
    return (interval % 2) * (intervals // 2) + interval // 2


def interval_at(rank, intervals):
    half = intervals // 2
    return lax.rem(rank, half) * 2 + rank // half


def host_of(window, interval, space, intervals):
    stride = space // intervals
    return (rank_of(interval, intervals) * stride + (window % 2) % stride) % space


def distances(space, intervals):
    stride = space // intervals
    return [0] + sorted(range(1, space), key=lambda turn: turn % stride == 0)


def away(host, turn, window, space):
    return (host + (turn if window % 2 == 0 else -turn)) % space


class Place:
    def __init__(self, space, intervals):
        stride = space // intervals
        self.window = lax.axis_index("tm")
        self.space = space
        self.sign = 1 - 2 * lax.rem(self.window, 2)
        self.position = lax.axis_index("space")
        shifted = lax.rem(
            self.position - lax.rem(lax.rem(self.window, 2), stride) + space, space
        )
        self.active = lax.rem(shifted, stride) == 0
        self.interval = interval_at(shifted // stride, intervals)
        below = shifted // stride
        above = lax.rem((shifted + stride - 1) // stride, intervals)
        self.nearest = jnp.where(self.sign > 0, below, above)
        self.number = self.window * intervals + self.interval


    def away(self, turn):
        return lax.rem(self.position + self.sign * turn + self.space, self.space)


def over_pairs(parts, body):
    if parts <= 8:
        for pair in range(parts // 2):
            body(pair)
    else:

        @pl.loop(0, parts // 2)
        def _(pair):
            body(pair)


class Sweeper:
    def __init__(self, parts, faces, gather, listing, aux, outs, work):
        self.parts, self.faces = parts, faces
        self.gather, self.listing, self.aux = gather, listing, aux
        self.outs, self.work = outs, work

    def clear_rim(self):
        zero = jnp.zeros((ROWS, LANES), BF)
        self.outs[0] = zero
        self.outs[self.parts + 1] = zero

    def set_drive(self, state, decay_row, forcing=None):
        def body(pair):
            for side in range(2):
                part = 2 * pair + side
                drive = state[part].astype(F32) * self.aux[part, decay_row : decay_row + 1, :]
                if forcing is not None:
                    drive = drive + forcing(part).astype(F32)
                self.work[
                    pair, self.faces * ROWS :, side * LANES : (side + 1) * LANES
                ] = drive.astype(BF)

        over_pairs(self.parts, body)

    def sweep(self, source, target, table, extra=None):
        lane = lax.broadcasted_iota(jnp.int32, (ROWS, LANES), 1)

        def listed(pair):
            both = jnp.concatenate([source[2 * pair], source[2 * pair + 1]], axis=1)
            chosen = dot(both, self.listing[pair]).astype(BF)
            self.outs[2 * pair + 1] = chosen[:, :LANES]
            self.outs[2 * pair + 2] = chosen[:, LANES:]

        def gathered(pair):
            for side in range(2):
                part = 2 * pair + side
                rim = jnp.where(lane < LANES // 2, self.outs[part], self.outs[part + 2])
                own = source[part]
                found = dot(jnp.concatenate([own, rim], axis=1), self.gather[part]).astype(BF)
                own, rim = own.astype(F32), rim.astype(F32)
                for face in range(self.faces):
                    if face < self.faces - PICKED:
                        value = found[:, face * LANES : (face + 1) * LANES]
                    else:
                        row = 3 + face - (self.faces - PICKED)
                        place = jnp.broadcast_to(
                            self.aux[part, row : row + 1, :].astype(jnp.int32), (ROWS, LANES)
                        )
                        lanes = place & (LANES - 1)
                        inner = jnp.where(place < 0, 0.0, jnp.take_along_axis(own, lanes, axis=1))
                        outer = jnp.take_along_axis(rim, lanes, axis=1)
                        value = jnp.where(place < LANES, inner, outer).astype(BF)
                    self.work[
                        pair,
                        face * ROWS : (face + 1) * ROWS,
                        side * LANES : (side + 1) * LANES,
                    ] = value

        def applied(pair):
            both = dot(table[...], self.work[pair])
            for side in range(2):
                part = 2 * pair + side
                result = both[:, side * LANES : (side + 1) * LANES]
                prism = jnp.concatenate(
                    [result[ROWS:], jnp.zeros((ROWS - PROWS, LANES), F32)], axis=0
                )
                kind = self.aux[part, 0:1, :]
                value = jnp.where(kind == 0.0, result[:ROWS], prism)
                if extra is not None:
                    value = value + extra[part].astype(F32)
                target[part] = value.astype(BF)

        over_pairs(self.parts, listed)
        over_pairs(self.parts, gathered)
        over_pairs(self.parts, applied)

    def step(self, state, other, table, decay_row, forcing=None, extra=None):
        self.set_drive(state, decay_row, forcing)
        places = [state, other]
        for turn in range(SWEEPS):
            last = turn + 1 == SWEEPS
            self.sweep(
                places[turn % 2], places[(turn + 1) % 2], table, extra if last else None
            )


def pack_kernel(space, intervals, etype, *refs):
    sources, refs = refs[:5], refs[5:]
    messages, refs = refs[:intervals], refs[intervals:]
    held, (wide, packed, in_sem, out_sem) = refs[:5], refs[5:]
    arriving = []
    for index in range(5):
        arriving.append(pltpu.make_async_copy(sources[index], held[index], in_sem.at[index]))
        arriving[-1].start()
    for copy in arriving:
        copy.wait()
    forcing, initial, damping, send_index, conn = held
    steps = forcing.shape[1]
    wide[...] = forcing[...].astype(F32).reshape(wide.shape)
    place = Place(space, intervals)
    width = initial.shape[0]
    faces = conn.shape[0]
    lists = pltpu.roll(jnp.broadcast_to(send_index[...].astype(F32), (8, LANES)), LANES // 2, 1)
    kinds = jnp.broadcast_to(etype[0].astype(F32), (1, LANES))
    first = jnp.concatenate([conn[...].astype(F32), kinds, lists[:1]], axis=0).astype(BF)
    rest = damping[...]
    pieces = []
    for _ in range(3):
        pieces.append(rest.astype(BF))
        rest = rest - pieces[-1].astype(F32)
    second = jnp.concatenate(pieces, axis=0)
    leaving = []
    for turn in range(intervals):
        rank = lax.rem(place.nearest - place.sign * turn + intervals, intervals)
        interval = interval_at(rank, intervals)
        out = packed.at[turn]
        for index in range(COARSEN):
            rows = pl.ds(interval * COARSEN + index, width, stride=steps)
            out[index, :width] = wide[rows, :].astype(BF)
        out[COARSEN, :width] = initial[...]
        out[0, width : width + faces + 2] = first
        out[1, width : width + 3] = second
        leaving.append(pltpu.make_async_copy(out, messages[turn], out_sem.at[turn]))
        leaving[-1].start()
    for copy in leaving:
        copy.wait()


def fine_kernel(space, intervals, width, faces, *refs):
    messages = refs[:space]
    table, residual, gather, listing, aux, forcing, start = refs[space : space + 7]
    other, outs, work = refs[space + 7 :]
    place = Place(space, intervals)

    @pl.when(place.active)
    def _():
        sweeper = Sweeper(space, faces, gather, listing, aux, outs, work)
        sweeper.clear_rim()
        rows = lax.broadcasted_iota(jnp.int32, (ROWS, LANES), 0).astype(F32)
        full = lax.broadcasted_iota(jnp.int32, (2 * LANES, LANES), 0).astype(F32)
        half = full[:LANES]
        zero = jnp.zeros((LANES, LANES), BF)
        for turn in range(space):
            part = place.away(turn)
            message = messages[turn]
            for index in range(COARSEN):
                forcing[part, index] = message[index]
            first = message[0, width : width + faces + 2].astype(F32)
            second = message[1, width : width + 3].astype(F32)
            kind = first[faces : faces + 1]
            damping = (second[0:1] + second[1:2]) + second[2:3]
            picked = [first[face : face + 1] for face in range(faces - PICKED, faces)]
            picked[-1] = jnp.where(kind == 0.0, picked[-1], -1.0)
            aux[part] = jnp.concatenate(
                [
                    kind,
                    jnp.exp(-damping),
                    jnp.exp(-COARSEN * damping),
                    *picked,
                    jnp.zeros((5 - PICKED, LANES), F32),
                ],
                axis=0,
            )
            for face in range(faces - PICKED):
                found = full == first[face : face + 1]
                gather[part, :, face * LANES : (face + 1) * LANES] = jnp.where(
                    found, 1.0, 0.0
                ).astype(BF)
            picks = jnp.where(half == first[faces + 1 : faces + 2], 1.0, 0.0).astype(BF)
            odd = lax.rem(part, 2) == 1
            left = jnp.where(odd, 0.0, 1.0).astype(BF)
            right = jnp.where(odd, 1.0, 0.0).astype(BF)
            listing[part // 2, pl.ds(pl.multiple_of(lax.rem(part, 2) * LANES, LANES), LANES), :] = (
                jnp.concatenate([picks * left, picks * right], axis=1)
            )
            limit = jnp.where(kind == 0.0, float(width), float(PRISM))
            wanted = (rows < limit) & (place.number == 0)
            start[part] = jnp.where(wanted, message[COARSEN].astype(F32), 0.0).astype(BF)

        residual[...] = start[...]

        @pl.loop(0, COARSEN)
        def _(index):
            sweeper.step(residual, other, table, 1, lambda part: forcing[part, index])


def added(first, second):
    return (first.astype(F32) + second.astype(F32)).astype(BF)


def horner(sweeper, state, other, table, terms, known):
    for index, term in enumerate(terms):

        @pl.when(known + index >= 0)
        def _():
            sweeper.step(state, other, table, 2, extra=term)

        @pl.when(known + index < 0)
        def _():
            state[...] = term[...]


def near_kernel(space, intervals, windows, faces, *refs):
    terms = refs[:intervals]
    table, gather, listing, aux, result, other, outs, work = refs[intervals:]
    place = Place(space, intervals)

    @pl.when(place.active & (place.window + 1 < windows))
    def _():
        sweeper = Sweeper(space, faces, gather, listing, aux, outs, work)
        sweeper.clear_rim()
        result[...] = terms[0][...]
        horner(sweeper, result, other, table, terms[1:], place.number - intervals)


def far_kernel(space, intervals, least, faces, *refs):
    *terms, table, gather, listing, aux, result, other, outs, work = refs
    place = Place(space, intervals)

    @pl.when(place.active & (place.window >= least))
    def _():
        sweeper = Sweeper(space, faces, gather, listing, aux, outs, work)
        sweeper.clear_rim()
        result[...] = added(terms[0][...], terms[1][...]) if len(terms) > 1 else terms[0][...]

        @pl.loop(0, intervals)
        def _(turn):
            sweeper.step(result, other, table, 2)

    @pl.when(place.window < least)
    def _():
        result[...] = jnp.zeros(result.shape, BF)


def final_kernel(space, intervals, width, faces, *refs):
    near, refs = refs[:intervals], refs[intervals:]
    earlier, inner, residual, start, forcing = refs[:5]
    fine_table, coarse_table, gather, listing, aux = refs[5:10]
    pieces = refs[10 : 10 + space]
    before, states, other, outs, work = refs[10 + space :]
    place = Place(space, intervals)

    @pl.when(place.active)
    def _():
        sweeper = Sweeper(space, faces, gather, listing, aux, outs, work)
        sweeper.clear_rim()
        before[...] = added(earlier[...], inner[...])
        horner(sweeper, before, other, coarse_table, near, place.number - intervals - 1)
        last = COARSEN - 1
        state = states.at[last]
        state[...] = before[...]
        sweeper.step(state, other, coarse_table, 2, extra=residual)
        first = place.number == 0
        states[0] = jnp.where(first, start[...], before[...])

        @pl.loop(0, last)
        def _(index):
            now = states.at[index]
            sweeper.step(now, other, fine_table, 1, lambda part: forcing[part, index])

            @pl.when(index + 1 < last)
            def _():
                states[index + 1] = now[...]

        for turn in range(space):
            part = place.away(turn)
            for index in range(COARSEN):
                pieces[turn][index] = states[index, part][:width]


def gather_kernel(space, intervals, *refs):
    pieces = dict(zip(distances(space, intervals), refs))
    out, sem = refs[space:]
    stride = space // intervals
    place = Place(space, intervals)
    offset = lax.rem(lax.rem(place.window, 2), stride)
    for interval in range(intervals):
        host = rank_of(interval, intervals) * stride + offset
        wanted = lax.rem(place.sign * (place.position - host) + 2 * space, space)
        for turn in range(space):

            @pl.when(wanted == turn)
            def _():
                pltpu.make_async_copy(
                    pieces[turn], out.at[pl.ds(interval * COARSEN, COARSEN)], sem.at[interval]
                ).start()

    for interval in range(intervals):
        pltpu.make_async_copy(
            pieces[0], out.at[pl.ds(interval * COARSEN, COARSEN)], sem.at[interval]
        ).wait()


def fold_kernel(fine, coarse, coupling, fine_table, coarse_table, wide):
    faces, width, _ = coupling.shape
    wide[...] = jnp.zeros(wide.shape, F32)
    for face in range(faces):
        wide[:width, face * ROWS : face * ROWS + width] = -coupling[face].astype(F32)
    rows = lax.broadcasted_iota(jnp.int32, (width, width), 0)
    columns = lax.broadcasted_iota(jnp.int32, (width, width), 1)
    wide[:width, faces * ROWS : faces * ROWS + width] = jnp.where(rows == columns, 1.0, 0.0)
    factors = wide[:width].astype(BF)
    for inverse, table in ((fine, fine_table), (coarse, coarse_table)):
        table[...] = jnp.zeros(table.shape, BF)
        table[:width] = dot(inverse[0], factors).astype(BF)
        table[ROWS : ROWS + PRISM] = dot(inverse[1], factors)[:PRISM].astype(BF)


def shards(initial, forcing, damping, block_inv, coarse_inv, coupling, etype, send_index, conn):
    width, elems = initial.shape
    faces = conn.shape[0]
    steps = forcing.shape[0]
    intervals = steps // COARSEN
    space = lax.axis_size("space")
    windows = lax.axis_size("tm")
    stride = space // intervals
    params = pltpu.CompilerParams(vmem_limit_bytes=min(56, 2 * space) * MIB)
    state_shape = jax.ShapeDtypeStruct((space, ROWS, LANES), BF)

    hbm = pl.BlockSpec(memory_space=pltpu.HBM)
    packing = [jnp.transpose(forcing, (1, 0, 2)), initial, damping[None], send_index[None], conn]
    message_shape = jax.ShapeDtypeStruct((COARSEN + 1, ROWS, LANES), BF)
    messages = pl.pallas_call(
        functools.partial(pack_kernel, space, intervals),
        out_shape=[message_shape] * intervals,
        in_specs=[pl.BlockSpec(memory_space=pltpu.SMEM)] + [hbm] * 5,
        out_specs=[hbm] * intervals,
        scratch_shapes=[pltpu.VMEM(array.shape, array.dtype) for array in packing]
        + [
            pltpu.VMEM((width * steps, LANES), F32),
            pltpu.VMEM((intervals, COARSEN + 1, ROWS, LANES), BF),
            pltpu.SemaphoreType.DMA((5,)),
            pltpu.SemaphoreType.DMA((intervals,)),
        ],
        compiler_params=pltpu.CompilerParams(vmem_limit_bytes=60 * MIB),
        name="pack",
    )(etype, *packing)

    received = [messages[0]] * space
    for turn in range(1, space):
        pairs = []
        for window in range(windows):
            for interval in range(intervals):
                host = host_of(window, interval, space, intervals)
                source = away(host, turn, window, space)
                pairs.append((window * space + source, window * space + host))
        received[turn] = lax.ppermute(messages[turn // stride], ("tm", "space"), pairs)

    table_shape = jax.ShapeDtypeStruct((ROWS + PROWS, (faces + 1) * ROWS), BF)
    fine_table, coarse_table = pl.pallas_call(
        fold_kernel,
        out_shape=[table_shape] * 2,
        in_specs=[VMEM] * 3,
        out_specs=[VMEM] * 2,
        scratch_shapes=[pltpu.VMEM((ROWS, (faces + 1) * ROWS), F32)],
        compiler_params=params,
        name="fold",
    )(block_inv, coarse_inv, coupling)

    gather_shape = jax.ShapeDtypeStruct((space, 2 * LANES, (faces - PICKED) * LANES), BF)
    listing_shape = jax.ShapeDtypeStruct((space // 2, 2 * LANES, 2 * LANES), BF)
    aux_shape = jax.ShapeDtypeStruct((space, 8, LANES), F32)
    forcing_shape = jax.ShapeDtypeStruct((space, COARSEN, ROWS, LANES), BF)
    scratch = [
        pltpu.VMEM((space, ROWS, LANES), BF),
        pltpu.VMEM((space + 2, ROWS, LANES), BF),
        pltpu.VMEM((space // 2, (faces + 1) * ROWS, 2 * LANES), BF),
    ]
    residual, gather, listing, aux, whole_forcing, start = pl.pallas_call(
        functools.partial(fine_kernel, space, intervals, width, faces),
        out_shape=[state_shape, gather_shape, listing_shape, aux_shape, forcing_shape, state_shape],
        in_specs=[VMEM] * (space + 1),
        out_specs=[VMEM] * 6,
        scratch_shapes=scratch,
        compiler_params=params,
        name="fine",
    )(*received, fine_table)

    def from_earlier(value, by):
        pairs = []
        for number in range(by, windows * intervals):
            target = number // intervals
            source = (number - by) // intervals
            pairs.append(
                (
                    source * space + host_of(source, (number - by) % intervals, space, intervals),
                    target * space + host_of(target, number % intervals, space, intervals),
                )
            )
        return lax.ppermute(value, ("tm", "space"), pairs)

    def chain(kernel, number, terms, name):
        return pl.pallas_call(
            functools.partial(kernel, space, intervals, number, faces),
            out_shape=state_shape,
            in_specs=[VMEM] * (len(terms) + 4),
            out_specs=VMEM,
            scratch_shapes=scratch,
            compiler_params=params,
            name=name,
        )(*terms, coarse_table, gather, listing, aux)

    near = [from_earlier(residual, by) for by in range(intervals, 0, -1)]
    partial = chain(near_kernel, windows, near, "near")
    earlier, *inner = [
        from_earlier(partial, by * intervals) for by in range(windows - 1, 0, -1)
    ]
    earlier = chain(far_kernel, windows - 1, [earlier], "far")
    for index, term in enumerate(inner[:-1]):
        earlier = chain(far_kernel, windows - 2 - index, [earlier, term], "far")

    piece_shape = jax.ShapeDtypeStruct((COARSEN, width, LANES), BF)
    pieces = pl.pallas_call(
        functools.partial(final_kernel, space, intervals, width, faces),
        out_shape=[piece_shape] * space,
        in_specs=[VMEM] * (intervals + 10),
        out_specs=[VMEM] * space,
        scratch_shapes=[
            pltpu.VMEM((space, ROWS, LANES), BF),
            pltpu.VMEM((COARSEN, space, ROWS, LANES), BF),
        ]
        + scratch,
        compiler_params=params,
        name="final",
    )(
        *near,
        earlier,
        inner[-1],
        residual,
        start,
        whole_forcing,
        fine_table,
        coarse_table,
        gather,
        listing,
        aux,
    )

    returned = [pieces[0]] * space
    turns = distances(space, intervals)
    for turn in turns[1:]:
        pairs = []
        for window in range(windows):
            for interval in range(intervals):
                host = host_of(window, interval, space, intervals)
                target = away(host, turn, window, space)
                pairs.append((window * space + host, window * space + target))
        returned[turn] = lax.ppermute(pieces[turn], ("tm", "space"), pairs)

    return pl.pallas_call(
        functools.partial(gather_kernel, space, intervals),
        out_shape=jax.ShapeDtypeStruct(forcing.shape, BF),
        in_specs=[pl.BlockSpec(memory_space=pl.ANY)] * space,
        out_specs=VMEM,
        scratch_shapes=[pltpu.SemaphoreType.DMA((intervals,))],
        compiler_params=params,
        name="place",
    )(*[returned[turn] for turn in turns])


def solution(mesh):
    in_specs = (
        P(None, "space"),
        P("tm", None, "space"),
        P("space"),
        P(),
        P(),
        P(),
        P("space"),
        P("space"),
        P(None, "space"),
    )
    out_specs = P("tm", None, "space")
    return jax.shard_map(shards, mesh=mesh, in_specs=in_specs, out_specs=out_specs, check_vma=False)
```

```python
import functools

import jax
import jax.numpy as jnp
from jax import lax
from jax.experimental import pallas as pl
from jax.experimental.pallas import tpu as pltpu
from jax.sharding import PartitionSpec as P

PRISM = 90
SWEEPS = 2
COARSEN = 4
ROWS = 144
PROWS = 96
LANES = 128
PICKED = 2
BF = jnp.bfloat16
F32 = jnp.float32
VMEM = pl.BlockSpec(memory_space=pltpu.VMEM)
MIB = 1024 * 1024


def dot(a, b):
    return jnp.dot(a, b, preferred_element_type=F32)


def rank_of(interval, intervals):
    return (interval % 2) * (intervals // 2) + interval // 2


def interval_at(rank, intervals):
    half = intervals // 2
    return lax.rem(rank, half) * 2 + rank // half


def host_of(window, interval, space, intervals):
    stride = space // intervals
    return (rank_of(interval, intervals) * stride + (window % 2) % stride) % space


def distances(space, intervals):
    stride = space // intervals
    return [0] + sorted(range(1, space), key=lambda turn: turn % stride == 0)


def away(host, turn, window, space):
    return (host + (turn if window % 2 == 0 else -turn)) % space


class Place:
    def __init__(self, space, intervals):
        stride = space // intervals
        self.window = lax.axis_index("tm")
        self.space = space
        self.sign = 1 - 2 * lax.rem(self.window, 2)
        self.position = lax.axis_index("space")
        shifted = lax.rem(
            self.position - lax.rem(lax.rem(self.window, 2), stride) + space, space
        )
        self.active = lax.rem(shifted, stride) == 0
        self.interval = interval_at(shifted // stride, intervals)
        below = shifted // stride
        above = lax.rem((shifted + stride - 1) // stride, intervals)
        self.nearest = jnp.where(self.sign > 0, below, above)
        self.number = self.window * intervals + self.interval


    def away(self, turn):
        return lax.rem(self.position + self.sign * turn + self.space, self.space)


def over_pairs(parts, body):
    if parts <= 8:
        for pair in range(parts // 2):
            body(pair)
    else:

        @pl.loop(0, parts // 2)
        def _(pair):
            body(pair)


class Sweeper:
    def __init__(self, parts, faces, gather, listing, aux, outs, work):
        self.parts, self.faces = parts, faces
        self.gather, self.listing, self.aux = gather, listing, aux
        self.outs, self.work = outs, work

    def clear_rim(self):
        zero = jnp.zeros((ROWS, LANES), BF)
        self.outs[0] = zero
        self.outs[self.parts + 1] = zero

    def set_drive(self, state, decay_row, forcing=None):
        def body(pair):
            for side in range(2):
                part = 2 * pair + side
                drive = state[part].astype(F32) * self.aux[part, decay_row : decay_row + 1, :]
                if forcing is not None:
                    drive = drive + forcing(part).astype(F32)
                self.work[
                    pair, self.faces * ROWS :, side * LANES : (side + 1) * LANES
                ] = drive.astype(BF)

        over_pairs(self.parts, body)

    def sweep(self, source, target, table, extra=None):
        lane = lax.broadcasted_iota(jnp.int32, (ROWS, LANES), 1)

        def listed(pair):
            both = jnp.concatenate([source[2 * pair], source[2 * pair + 1]], axis=1)
            chosen = dot(both, self.listing[pair]).astype(BF)
            self.outs[2 * pair + 1] = chosen[:, :LANES]
            self.outs[2 * pair + 2] = chosen[:, LANES:]

        def gathered(pair):
            for side in range(2):
                part = 2 * pair + side
                rim = jnp.where(lane < LANES // 2, self.outs[part], self.outs[part + 2])
                own = source[part]
                found = dot(jnp.concatenate([own, rim], axis=1), self.gather[part]).astype(BF)
                own, rim = own.astype(F32), rim.astype(F32)
                for face in range(self.faces):
                    if face < self.faces - PICKED:
                        value = found[:, face * LANES : (face + 1) * LANES]
                    else:
                        row = 3 + face - (self.faces - PICKED)
                        place = jnp.broadcast_to(
                            self.aux[part, row : row + 1, :].astype(jnp.int32), (ROWS, LANES)
                        )
                        lanes = place & (LANES - 1)
                        inner = jnp.where(place < 0, 0.0, jnp.take_along_axis(own, lanes, axis=1))
                        outer = jnp.take_along_axis(rim, lanes, axis=1)
                        value = jnp.where(place < LANES, inner, outer).astype(BF)
                    self.work[
                        pair,
                        face * ROWS : (face + 1) * ROWS,
                        side * LANES : (side + 1) * LANES,
                    ] = value

        def applied(pair):
            both = dot(table[...], self.work[pair])
            for side in range(2):
                part = 2 * pair + side
                result = both[:, side * LANES : (side + 1) * LANES]
                prism = jnp.concatenate(
                    [result[ROWS:], jnp.zeros((ROWS - PROWS, LANES), F32)], axis=0
                )
                kind = self.aux[part, 0:1, :]
                value = jnp.where(kind == 0.0, result[:ROWS], prism)
                if extra is not None:
                    value = value + extra[part].astype(F32)
                target[part] = value.astype(BF)

        over_pairs(self.parts, listed)
        over_pairs(self.parts, gathered)
        over_pairs(self.parts, applied)

    def step(self, state, other, table, decay_row, forcing=None, extra=None):
        self.set_drive(state, decay_row, forcing)
        places = [state, other]
        for turn in range(SWEEPS):
            last = turn + 1 == SWEEPS
            self.sweep(
                places[turn % 2], places[(turn + 1) % 2], table, extra if last else None
            )


def pack_kernel(space, intervals, etype, *refs):
    sources, refs = refs[:5], refs[5:]
    messages, refs = refs[:intervals], refs[intervals:]
    held, (wide, packed, in_sem, out_sem) = refs[:5], refs[5:]
    arriving = []
    for index in range(5):
        arriving.append(pltpu.make_async_copy(sources[index], held[index], in_sem.at[index]))
        arriving[-1].start()
    for copy in arriving:
        copy.wait()
    forcing, initial, damping, send_index, conn = held
    steps = forcing.shape[1]
    lines = forcing.shape[0] * steps
    wide[:lines] = forcing[...].astype(F32).reshape(lines, LANES)
    place = Place(space, intervals)
    width = initial.shape[0]
    faces = conn.shape[0]
    lists = pltpu.roll(jnp.broadcast_to(send_index[...].astype(F32), (8, LANES)), LANES // 2, 1)
    kinds = jnp.broadcast_to(etype[0].astype(F32), (1, LANES))
    first = jnp.concatenate([conn[...].astype(F32), kinds, lists[:1]], axis=0).astype(BF)
    rest = damping[...]
    pieces = []
    for _ in range(3):
        pieces.append(rest.astype(BF))
        rest = rest - pieces[-1].astype(F32)
    second = jnp.concatenate(pieces, axis=0)
    leaving = []
    for turn in range(intervals):
        rank = lax.rem(place.nearest - place.sign * turn + intervals, intervals)
        interval = interval_at(rank, intervals)
        out = packed.at[turn]
        for index in range(COARSEN):
            rows = pl.ds(interval * COARSEN + index, width, stride=steps)
            out[index, :width] = wide[rows, :].astype(BF)
        out[COARSEN, :width] = initial[...]
        out[0, width : width + faces + 2] = first
        out[1, width : width + 3] = second
        leaving.append(pltpu.make_async_copy(out, messages[turn], out_sem.at[turn]))
        leaving[-1].start()
    for copy in leaving:
        copy.wait()


def fine_kernel(space, intervals, width, faces, *refs):
    messages = refs[:space]
    table, residual, gather, listing, aux, forcing, start = refs[space : space + 7]
    other, outs, work = refs[space + 7 :]
    place = Place(space, intervals)

    @pl.when(place.active)
    def _():
        sweeper = Sweeper(space, faces, gather, listing, aux, outs, work)
        sweeper.clear_rim()
        rows = lax.broadcasted_iota(jnp.int32, (ROWS, LANES), 0).astype(F32)
        full = lax.broadcasted_iota(jnp.int32, (2 * LANES, LANES), 0).astype(F32)
        half = full[:LANES]
        zero = jnp.zeros((LANES, LANES), BF)
        for turn in range(space):
            part = place.away(turn)
            message = messages[turn]
            for index in range(COARSEN):
                forcing[part, index] = message[index]
            first = message[0, width : width + faces + 2].astype(F32)
            second = message[1, width : width + 3].astype(F32)
            kind = first[faces : faces + 1]
            damping = (second[0:1] + second[1:2]) + second[2:3]
            picked = [first[face : face + 1] for face in range(faces - PICKED, faces)]
            picked[-1] = jnp.where(kind == 0.0, picked[-1], -1.0)
            aux[part] = jnp.concatenate(
                [
                    kind,
                    jnp.exp(-damping),
                    jnp.exp(-COARSEN * damping),
                    *picked,
                    jnp.zeros((5 - PICKED, LANES), F32),
                ],
                axis=0,
            )
            for face in range(faces - PICKED):
                found = full == first[face : face + 1]
                gather[part, :, face * LANES : (face + 1) * LANES] = jnp.where(
                    found, 1.0, 0.0
                ).astype(BF)
            picks = jnp.where(half == first[faces + 1 : faces + 2], 1.0, 0.0).astype(BF)
            odd = lax.rem(part, 2) == 1
            left = jnp.where(odd, 0.0, 1.0).astype(BF)
            right = jnp.where(odd, 1.0, 0.0).astype(BF)
            listing[part // 2, pl.ds(pl.multiple_of(lax.rem(part, 2) * LANES, LANES), LANES), :] = (
                jnp.concatenate([picks * left, picks * right], axis=1)
            )
            limit = jnp.where(kind == 0.0, float(width), float(PRISM))
            wanted = (rows < limit) & (place.number == 0)
            start[part] = jnp.where(wanted, message[COARSEN].astype(F32), 0.0).astype(BF)

        residual[...] = start[...]

        @pl.loop(0, COARSEN)
        def _(index):
            sweeper.step(residual, other, table, 1, lambda part: forcing[part, index])


def added(first, second):
    return (first.astype(F32) + second.astype(F32)).astype(BF)


def horner(sweeper, state, other, table, terms, known):
    for index, term in enumerate(terms):

        @pl.when(known + index >= 0)
        def _():
            sweeper.step(state, other, table, 2, extra=term)

        @pl.when(known + index < 0)
        def _():
            state[...] = term[...]


def near_kernel(space, intervals, windows, faces, *refs):
    terms = refs[:intervals]
    table, gather, listing, aux, result, other, outs, work = refs[intervals:]
    place = Place(space, intervals)

    @pl.when(place.active & (place.window + 1 < windows))
    def _():
        sweeper = Sweeper(space, faces, gather, listing, aux, outs, work)
        sweeper.clear_rim()
        result[...] = terms[0][...]
        horner(sweeper, result, other, table, terms[1:], place.number - intervals)


def far_kernel(space, intervals, least, faces, *refs):
    *terms, table, gather, listing, aux, result, other, outs, work = refs
    place = Place(space, intervals)

    @pl.when(place.active & (place.window >= least))
    def _():
        sweeper = Sweeper(space, faces, gather, listing, aux, outs, work)
        sweeper.clear_rim()
        result[...] = added(terms[0][...], terms[1][...]) if len(terms) > 1 else terms[0][...]

        @pl.loop(0, intervals)
        def _(turn):
            sweeper.step(result, other, table, 2)

    @pl.when(place.window < least)
    def _():
        result[...] = jnp.zeros(result.shape, BF)


def final_kernel(space, intervals, width, faces, *refs):
    near, refs = refs[:intervals], refs[intervals:]
    earlier, inner, residual, start, forcing = refs[:5]
    fine_table, coarse_table, gather, listing, aux = refs[5:10]
    pieces = refs[10 : 10 + space]
    before, states, other, outs, work = refs[10 + space :]
    place = Place(space, intervals)

    @pl.when(place.active)
    def _():
        sweeper = Sweeper(space, faces, gather, listing, aux, outs, work)
        sweeper.clear_rim()
        before[...] = added(earlier[...], inner[...])
        horner(sweeper, before, other, coarse_table, near, place.number - intervals - 1)
        last = COARSEN - 1
        state = states.at[last]
        state[...] = before[...]
        sweeper.step(state, other, coarse_table, 2, extra=residual)
        first = place.number == 0
        states[0] = jnp.where(first, start[...], before[...])

        @pl.loop(0, last)
        def _(index):
            now = states.at[index]
            sweeper.step(now, other, fine_table, 1, lambda part: forcing[part, index])

            @pl.when(index + 1 < last)
            def _():
                states[index + 1] = now[...]

        for turn in range(space):
            part = place.away(turn)
            for index in range(COARSEN):
                pieces[turn][index] = states[index, part][:width]


def gather_kernel(space, intervals, *refs):
    pieces = dict(zip(distances(space, intervals), refs))
    out, sem = refs[space:]
    stride = space // intervals
    place = Place(space, intervals)
    offset = lax.rem(lax.rem(place.window, 2), stride)
    for interval in range(intervals):
        host = rank_of(interval, intervals) * stride + offset
        wanted = lax.rem(place.sign * (place.position - host) + 2 * space, space)
        for turn in range(space):

            @pl.when(wanted == turn)
            def _():
                pltpu.make_async_copy(
                    pieces[turn], out.at[pl.ds(interval * COARSEN, COARSEN)], sem.at[interval]
                ).start()

    for interval in range(intervals):
        pltpu.make_async_copy(
            pieces[0], out.at[pl.ds(interval * COARSEN, COARSEN)], sem.at[interval]
        ).wait()


def fold_kernel(fine, coarse, coupling, fine_table, coarse_table, wide):
    faces, width, _ = coupling.shape
    wide[...] = jnp.zeros(wide.shape, F32)
    for face in range(faces):
        wide[:width, face * ROWS : face * ROWS + width] = -coupling[face].astype(F32)
    rows = lax.broadcasted_iota(jnp.int32, (width, width), 0)
    columns = lax.broadcasted_iota(jnp.int32, (width, width), 1)
    wide[:width, faces * ROWS : faces * ROWS + width] = jnp.where(rows == columns, 1.0, 0.0)
    factors = wide[:width].astype(BF)
    for inverse, table in ((fine, fine_table), (coarse, coarse_table)):
        table[...] = jnp.zeros(table.shape, BF)
        table[:width] = dot(inverse[0], factors).astype(BF)
        table[ROWS : ROWS + PRISM] = dot(inverse[1], factors)[:PRISM].astype(BF)


def shards(initial, forcing, damping, block_inv, coarse_inv, coupling, etype, send_index, conn):
    width, elems = initial.shape
    faces = conn.shape[0]
    steps = forcing.shape[0]
    intervals = steps // COARSEN
    space = lax.axis_size("space")
    windows = lax.axis_size("tm")
    stride = space // intervals
    params = pltpu.CompilerParams(vmem_limit_bytes=min(56, 2 * space) * MIB)
    state_shape = jax.ShapeDtypeStruct((space, ROWS, LANES), BF)

    hbm = pl.BlockSpec(memory_space=pltpu.HBM)
    packing = [jnp.transpose(forcing, (1, 0, 2)), initial, damping[None], send_index[None], conn]
    message_shape = jax.ShapeDtypeStruct((COARSEN + 1, ROWS, LANES), BF)
    messages = pl.pallas_call(
        functools.partial(pack_kernel, space, intervals),
        out_shape=[message_shape] * intervals,
        in_specs=[pl.BlockSpec(memory_space=pltpu.SMEM)] + [hbm] * 5,
        out_specs=[hbm] * intervals,
        scratch_shapes=[pltpu.VMEM(array.shape, array.dtype) for array in packing]
        + [
            pltpu.VMEM(((width + 1) * steps, LANES), F32),
            pltpu.VMEM((intervals, COARSEN + 1, ROWS, LANES), BF),
            pltpu.SemaphoreType.DMA((5,)),
            pltpu.SemaphoreType.DMA((intervals,)),
        ],
        compiler_params=pltpu.CompilerParams(vmem_limit_bytes=60 * MIB),
        name="pack",
    )(etype, *packing)

    received = [messages[0]] * space
    for turn in range(1, space):
        pairs = []
        for window in range(windows):
            for interval in range(intervals):
                host = host_of(window, interval, space, intervals)
                source = away(host, turn, window, space)
                pairs.append((window * space + source, window * space + host))
        received[turn] = lax.ppermute(messages[turn // stride], ("tm", "space"), pairs)

    table_shape = jax.ShapeDtypeStruct((ROWS + PROWS, (faces + 1) * ROWS), BF)
    fine_table, coarse_table = pl.pallas_call(
        fold_kernel,
        out_shape=[table_shape] * 2,
        in_specs=[VMEM] * 3,
        out_specs=[VMEM] * 2,
        scratch_shapes=[pltpu.VMEM((ROWS, (faces + 1) * ROWS), F32)],
        compiler_params=params,
        name="fold",
    )(block_inv, coarse_inv, coupling)

    gather_shape = jax.ShapeDtypeStruct((space, 2 * LANES, (faces - PICKED) * LANES), BF)
    listing_shape = jax.ShapeDtypeStruct((space // 2, 2 * LANES, 2 * LANES), BF)
    aux_shape = jax.ShapeDtypeStruct((space, 8, LANES), F32)
    forcing_shape = jax.ShapeDtypeStruct((space, COARSEN, ROWS, LANES), BF)
    scratch = [
        pltpu.VMEM((space, ROWS, LANES), BF),
        pltpu.VMEM((space + 2, ROWS, LANES), BF),
        pltpu.VMEM((space // 2, (faces + 1) * ROWS, 2 * LANES), BF),
    ]
    residual, gather, listing, aux, whole_forcing, start = pl.pallas_call(
        functools.partial(fine_kernel, space, intervals, width, faces),
        out_shape=[state_shape, gather_shape, listing_shape, aux_shape, forcing_shape, state_shape],
        in_specs=[VMEM] * (space + 1),
        out_specs=[VMEM] * 6,
        scratch_shapes=scratch,
        compiler_params=params,
        name="fine",
    )(*received, fine_table)

    def from_earlier(value, by):
        pairs = []
        for number in range(by, windows * intervals):
            target = number // intervals
            source = (number - by) // intervals
            pairs.append(
                (
                    source * space + host_of(source, (number - by) % intervals, space, intervals),
                    target * space + host_of(target, number % intervals, space, intervals),
                )
            )
        return lax.ppermute(value, ("tm", "space"), pairs)

    def chain(kernel, number, terms, name):
        return pl.pallas_call(
            functools.partial(kernel, space, intervals, number, faces),
            out_shape=state_shape,
            in_specs=[VMEM] * (len(terms) + 4),
            out_specs=VMEM,
            scratch_shapes=scratch,
            compiler_params=params,
            name=name,
        )(*terms, coarse_table, gather, listing, aux)

    near = [from_earlier(residual, by) for by in range(intervals, 0, -1)]
    partial = chain(near_kernel, windows, near, "near")
    earlier, *inner = [
        from_earlier(partial, by * intervals) for by in range(windows - 1, 0, -1)
    ]
    earlier = chain(far_kernel, windows - 1, [earlier], "far")
    for index, term in enumerate(inner[:-1]):
        earlier = chain(far_kernel, windows - 2 - index, [earlier, term], "far")

    piece_shape = jax.ShapeDtypeStruct((COARSEN, width, LANES), BF)
    pieces = pl.pallas_call(
        functools.partial(final_kernel, space, intervals, width, faces),
        out_shape=[piece_shape] * space,
        in_specs=[VMEM] * (intervals + 10),
        out_specs=[VMEM] * space,
        scratch_shapes=[
            pltpu.VMEM((space, ROWS, LANES), BF),
            pltpu.VMEM((COARSEN, space, ROWS, LANES), BF),
        ]
        + scratch,
        compiler_params=params,
        name="final",
    )(
        *near,
        earlier,
        inner[-1],
        residual,
        start,
        whole_forcing,
        fine_table,
        coarse_table,
        gather,
        listing,
        aux,
    )

    returned = [pieces[0]] * space
    turns = distances(space, intervals)
    for turn in turns[1:]:
        pairs = []
        for window in range(windows):
            for interval in range(intervals):
                host = host_of(window, interval, space, intervals)
                target = away(host, turn, window, space)
                pairs.append((window * space + host, window * space + target))
        returned[turn] = lax.ppermute(pieces[turn], ("tm", "space"), pairs)

    return pl.pallas_call(
        functools.partial(gather_kernel, space, intervals),
        out_shape=jax.ShapeDtypeStruct(forcing.shape, BF),
        in_specs=[pl.BlockSpec(memory_space=pl.ANY)] * space,
        out_specs=VMEM,
        scratch_shapes=[pltpu.SemaphoreType.DMA((intervals,))],
        compiler_params=params,
        name="place",
    )(*[returned[turn] for turn in turns])


def solution(mesh):
    in_specs = (
        P(None, "space"),
        P("tm", None, "space"),
        P("space"),
        P(),
        P(),
        P(),
        P("space"),
        P("space"),
        P(None, "space"),
    )
    out_specs = P("tm", None, "space")
    return jax.shard_map(shards, mesh=mesh, in_specs=in_specs, out_specs=out_specs, check_vma=False)
```

```python
import functools

import jax
import jax.numpy as jnp
from jax import lax
from jax.experimental import pallas as pl
from jax.experimental.pallas import tpu as pltpu
from jax.sharding import PartitionSpec as P

PRISM = 90
SWEEPS = 2
COARSEN = 4
ROWS = 144
PROWS = 96
LANES = 128
PICKED = 2
BF = jnp.bfloat16
F32 = jnp.float32
VMEM = pl.BlockSpec(memory_space=pltpu.VMEM)
MIB = 1024 * 1024


def dot(a, b):
    return jnp.dot(a, b, preferred_element_type=F32)


def rank_of(interval, intervals):
    return (interval % 2) * (intervals // 2) + interval // 2


def interval_at(rank, intervals):
    half = intervals // 2
    return lax.rem(rank, half) * 2 + rank // half


def host_of(window, interval, space, intervals):
    stride = space // intervals
    return (rank_of(interval, intervals) * stride + (window % 2) % stride) % space


def distances(space, intervals):
    stride = space // intervals
    return [0] + sorted(range(1, space), key=lambda turn: turn % stride == 0)


def away(host, turn, window, space):
    return (host + (turn if window % 2 == 0 else -turn)) % space


class Place:
    def __init__(self, space, intervals):
        stride = space // intervals
        self.window = lax.axis_index("tm")
        self.space = space
        self.sign = 1 - 2 * lax.rem(self.window, 2)
        self.position = lax.axis_index("space")
        shifted = lax.rem(
            self.position - lax.rem(lax.rem(self.window, 2), stride) + space, space
        )
        self.active = lax.rem(shifted, stride) == 0
        self.interval = interval_at(shifted // stride, intervals)
        below = shifted // stride
        above = lax.rem((shifted + stride - 1) // stride, intervals)
        self.nearest = jnp.where(self.sign > 0, below, above)
        self.number = self.window * intervals + self.interval


    def away(self, turn):
        return lax.rem(self.position + self.sign * turn + self.space, self.space)


def over_pairs(parts, body):
    if parts <= 8:
        for pair in range(parts // 2):
            body(pair)
    else:

        @pl.loop(0, parts // 2)
        def _(pair):
            body(pair)


class Sweeper:
    def __init__(self, parts, faces, gather, listing, aux, outs, work):
        self.parts, self.faces = parts, faces
        self.gather, self.listing, self.aux = gather, listing, aux
        self.outs, self.work = outs, work

    def clear_rim(self):
        zero = jnp.zeros((ROWS, LANES), BF)
        self.outs[0] = zero
        self.outs[self.parts + 1] = zero

    def set_drive(self, state, decay_row, forcing=None):
        def body(pair):
            for side in range(2):
                part = 2 * pair + side
                drive = state[part].astype(F32) * self.aux[part, decay_row : decay_row + 1, :]
                if forcing is not None:
                    drive = drive + forcing(part).astype(F32)
                self.work[
                    pair, self.faces * ROWS :, side * LANES : (side + 1) * LANES
                ] = drive.astype(BF)

        over_pairs(self.parts, body)

    def sweep(self, source, target, table, extra=None):
        lane = lax.broadcasted_iota(jnp.int32, (ROWS, LANES), 1)

        def listed(pair):
            both = jnp.concatenate([source[2 * pair], source[2 * pair + 1]], axis=1)
            chosen = dot(both, self.listing[pair]).astype(BF)
            self.outs[2 * pair + 1] = chosen[:, :LANES]
            self.outs[2 * pair + 2] = chosen[:, LANES:]

        def gathered(pair):
            for side in range(2):
                part = 2 * pair + side
                rim = jnp.where(lane < LANES // 2, self.outs[part], self.outs[part + 2])
                own = source[part]
                found = dot(jnp.concatenate([own, rim], axis=1), self.gather[part]).astype(BF)
                own, rim = own.astype(F32), rim.astype(F32)
                for face in range(self.faces):
                    if face < self.faces - PICKED:
                        value = found[:, face * LANES : (face + 1) * LANES]
                    else:
                        row = 3 + face - (self.faces - PICKED)
                        place = jnp.broadcast_to(
                            self.aux[part, row : row + 1, :].astype(jnp.int32), (ROWS, LANES)
                        )
                        lanes = place & (LANES - 1)
                        inner = jnp.where(place < 0, 0.0, jnp.take_along_axis(own, lanes, axis=1))
                        outer = jnp.take_along_axis(rim, lanes, axis=1)
                        value = jnp.where(place < LANES, inner, outer).astype(BF)
                    self.work[
                        pair,
                        face * ROWS : (face + 1) * ROWS,
                        side * LANES : (side + 1) * LANES,
                    ] = value

        def applied(pair):
            both = dot(table[...], self.work[pair])
            for side in range(2):
                part = 2 * pair + side
                result = both[:, side * LANES : (side + 1) * LANES]
                prism = jnp.concatenate(
                    [result[ROWS:], jnp.zeros((ROWS - PROWS, LANES), F32)], axis=0
                )
                kind = self.aux[part, 0:1, :]
                value = jnp.where(kind == 0.0, result[:ROWS], prism)
                if extra is not None:
                    value = value + extra[part].astype(F32)
                target[part] = value.astype(BF)

        over_pairs(self.parts, listed)
        over_pairs(self.parts, gathered)
        over_pairs(self.parts, applied)

    def step(self, state, other, table, decay_row, forcing=None, extra=None):
        self.set_drive(state, decay_row, forcing)
        places = [state, other]
        for turn in range(SWEEPS):
            last = turn + 1 == SWEEPS
            self.sweep(
                places[turn % 2], places[(turn + 1) % 2], table, extra if last else None
            )


def pack_kernel(space, intervals, etype, *refs):
    sources, refs = refs[:5], refs[5:]
    messages, refs = refs[:intervals], refs[intervals:]
    held, (wide, packed, in_sem, out_sem) = refs[:5], refs[5:]
    arriving = []
    for index in range(5):
        arriving.append(pltpu.make_async_copy(sources[index], held[index], in_sem.at[index]))
        arriving[-1].start()
    for copy in arriving:
        copy.wait()
    forcing, initial, damping, send_index, conn = held
    steps = forcing.shape[1]
    lines = forcing.shape[0] * steps
    wide[:lines] = forcing[...].astype(F32).reshape(lines, LANES)
    place = Place(space, intervals)
    width = initial.shape[0]
    faces = conn.shape[0]
    lists = pltpu.roll(jnp.broadcast_to(send_index[...].astype(F32), (8, LANES)), LANES // 2, 1)
    kinds = jnp.broadcast_to(etype[0].astype(F32), (1, LANES))
    first = jnp.concatenate([conn[...].astype(F32), kinds, lists[:1]], axis=0).astype(BF)
    rest = damping[...]
    pieces = []
    for _ in range(3):
        pieces.append(rest.astype(BF))
        rest = rest - pieces[-1].astype(F32)
    second = jnp.concatenate(pieces, axis=0)
    leaving = []
    for turn in range(intervals):
        rank = lax.rem(place.nearest - place.sign * turn + intervals, intervals)
        interval = interval_at(rank, intervals)
        out = packed.at[turn]
        for index in range(COARSEN):
            rows = pl.ds(interval * COARSEN + index, width, stride=steps)
            out[index, :width] = wide[rows, :].astype(BF)
        out[COARSEN, :width] = initial[...]
        out[0, width : width + faces + 2] = first
        out[1, width : width + 3] = second
        leaving.append(pltpu.make_async_copy(out, messages[turn], out_sem.at[turn]))
        leaving[-1].start()
    for copy in leaving:
        copy.wait()


def fine_kernel(space, intervals, width, faces, *refs):
    messages = refs[:space]
    table, residual, gather, listing, aux, forcing, start = refs[space : space + 7]
    other, outs, work = refs[space + 7 :]
    place = Place(space, intervals)

    @pl.when(place.active)
    def _():
        sweeper = Sweeper(space, faces, gather, listing, aux, outs, work)
        sweeper.clear_rim()
        rows = lax.broadcasted_iota(jnp.int32, (ROWS, LANES), 0).astype(F32)
        full = lax.broadcasted_iota(jnp.int32, (2 * LANES, LANES), 0).astype(F32)
        half = full[:LANES]
        zero = jnp.zeros((LANES, LANES), BF)
        for turn in range(space):
            part = place.away(turn)
            message = messages[turn]
            for index in range(COARSEN):
                forcing[part, index] = message[index]
            first = message[0, width : width + faces + 2].astype(F32)
            second = message[1, width : width + 3].astype(F32)
            kind = first[faces : faces + 1]
            damping = (second[0:1] + second[1:2]) + second[2:3]
            picked = [first[face : face + 1] for face in range(faces - PICKED, faces)]
            picked[-1] = jnp.where(kind == 0.0, picked[-1], -1.0)
            aux[part] = jnp.concatenate(
                [
                    kind,
                    jnp.exp(-damping),
                    jnp.exp(-COARSEN * damping),
                    *picked,
                    jnp.zeros((5 - PICKED, LANES), F32),
                ],
                axis=0,
            )
            for face in range(faces - PICKED):
                found = full == first[face : face + 1]
                gather[part, :, face * LANES : (face + 1) * LANES] = jnp.where(
                    found, 1.0, 0.0
                ).astype(BF)
            picks = jnp.where(half == first[faces + 1 : faces + 2], 1.0, 0.0).astype(BF)
            odd = lax.rem(part, 2) == 1
            left = jnp.where(odd, 0.0, 1.0).astype(BF)
            right = jnp.where(odd, 1.0, 0.0).astype(BF)
            listing[part // 2, pl.ds(pl.multiple_of(lax.rem(part, 2) * LANES, LANES), LANES), :] = (
                jnp.concatenate([picks * left, picks * right], axis=1)
            )
            limit = jnp.where(kind == 0.0, float(width), float(PRISM))
            wanted = (rows < limit) & (place.number == 0)
            start[part] = jnp.where(wanted, message[COARSEN].astype(F32), 0.0).astype(BF)

        residual[...] = start[...]

        @pl.loop(0, COARSEN)
        def _(index):
            sweeper.step(residual, other, table, 1, lambda part: forcing[part, index])


def added(first, second):
    return (first.astype(F32) + second.astype(F32)).astype(BF)


def horner(sweeper, state, other, table, terms, known):
    for index, term in enumerate(terms):

        @pl.when(known + index >= 0)
        def _():
            sweeper.step(state, other, table, 2, extra=term)

        @pl.when(known + index < 0)
        def _():
            state[...] = term[...]


def near_kernel(space, intervals, windows, faces, *refs):
    terms = refs[:intervals]
    table, gather, listing, aux, result, other, outs, work = refs[intervals:]
    place = Place(space, intervals)

    @pl.when(place.active & (place.window + 1 < windows))
    def _():
        sweeper = Sweeper(space, faces, gather, listing, aux, outs, work)
        sweeper.clear_rim()
        result[...] = terms[0][...]
        horner(sweeper, result, other, table, terms[1:], place.number - intervals)


def far_kernel(space, intervals, least, faces, *refs):
    *terms, table, gather, listing, aux, result, other, outs, work = refs
    place = Place(space, intervals)

    @pl.when(place.active & (place.window >= least))
    def _():
        sweeper = Sweeper(space, faces, gather, listing, aux, outs, work)
        sweeper.clear_rim()
        result[...] = added(terms[0][...], terms[1][...]) if len(terms) > 1 else terms[0][...]

        @pl.loop(0, intervals)
        def _(turn):
            sweeper.step(result, other, table, 2)

    @pl.when(place.window < least)
    def _():
        result[...] = jnp.zeros(result.shape, BF)


def final_kernel(space, intervals, width, faces, *refs):
    near, refs = refs[:intervals], refs[intervals:]
    earlier, inner, residual, start, forcing = refs[:5]
    fine_table, coarse_table, gather, listing, aux = refs[5:10]
    pieces = refs[10 : 10 + space]
    before, states, other, outs, work = refs[10 + space :]
    place = Place(space, intervals)

    @pl.when(place.active)
    def _():
        sweeper = Sweeper(space, faces, gather, listing, aux, outs, work)
        sweeper.clear_rim()
        before[...] = added(earlier[...], inner[...])
        horner(sweeper, before, other, coarse_table, near, place.number - intervals - 1)
        last = COARSEN - 1
        state = states.at[last]
        state[...] = before[...]
        sweeper.step(state, other, coarse_table, 2, extra=residual)
        first = place.number == 0
        states[0] = jnp.where(first, start[...], before[...])

        @pl.loop(0, last)
        def _(index):
            now = states.at[index]
            sweeper.step(now, other, fine_table, 1, lambda part: forcing[part, index])

            @pl.when(index + 1 < last)
            def _():
                states[index + 1] = now[...]

        for turn in range(space):
            part = place.away(turn)
            for index in range(COARSEN):
                pieces[turn][index] = states[index, part][:width]


def gather_kernel(space, intervals, *refs):
    pieces = dict(zip(distances(space, intervals), refs))
    out, sem = refs[space:]
    stride = space // intervals
    place = Place(space, intervals)
    offset = lax.rem(lax.rem(place.window, 2), stride)
    for interval in range(intervals):
        host = rank_of(interval, intervals) * stride + offset
        wanted = lax.rem(place.sign * (place.position - host) + 2 * space, space)
        for turn in range(space):

            @pl.when(wanted == turn)
            def _():
                pltpu.make_async_copy(
                    pieces[turn], out.at[pl.ds(interval * COARSEN, COARSEN)], sem.at[interval]
                ).start()

    for interval in range(intervals):
        pltpu.make_async_copy(
            pieces[0], out.at[pl.ds(interval * COARSEN, COARSEN)], sem.at[interval]
        ).wait()


def fold_kernel(fine, coarse, coupling, message, fine_table, coarse_table, own, wide):
    faces, width, _ = coupling.shape
    own[...] = message[...]
    wide[...] = jnp.zeros(wide.shape, F32)
    for face in range(faces):
        wide[:width, face * ROWS : face * ROWS + width] = -coupling[face].astype(F32)
    rows = lax.broadcasted_iota(jnp.int32, (width, width), 0)
    columns = lax.broadcasted_iota(jnp.int32, (width, width), 1)
    wide[:width, faces * ROWS : faces * ROWS + width] = jnp.where(rows == columns, 1.0, 0.0)
    factors = wide[:width].astype(BF)
    for inverse, table in ((fine, fine_table), (coarse, coarse_table)):
        table[...] = jnp.zeros(table.shape, BF)
        table[:width] = dot(inverse[0], factors).astype(BF)
        table[ROWS : ROWS + PRISM] = dot(inverse[1], factors)[:PRISM].astype(BF)


def shards(initial, forcing, damping, block_inv, coarse_inv, coupling, etype, send_index, conn):
    width, elems = initial.shape
    faces = conn.shape[0]
    steps = forcing.shape[0]
    intervals = steps // COARSEN
    space = lax.axis_size("space")
    windows = lax.axis_size("tm")
    stride = space // intervals
    params = pltpu.CompilerParams(vmem_limit_bytes=min(56, 2 * space) * MIB)
    state_shape = jax.ShapeDtypeStruct((space, ROWS, LANES), BF)

    hbm = pl.BlockSpec(memory_space=pltpu.HBM)
    packing = [jnp.transpose(forcing, (1, 0, 2)), initial, damping[None], send_index[None], conn]
    message_shape = jax.ShapeDtypeStruct((COARSEN + 1, ROWS, LANES), BF)
    messages = pl.pallas_call(
        functools.partial(pack_kernel, space, intervals),
        out_shape=[message_shape] * intervals,
        in_specs=[pl.BlockSpec(memory_space=pltpu.SMEM)] + [hbm] * 5,
        out_specs=[hbm] * intervals,
        scratch_shapes=[pltpu.VMEM(array.shape, array.dtype) for array in packing]
        + [
            pltpu.VMEM(((width + 1) * steps, LANES), F32),
            pltpu.VMEM((intervals, COARSEN + 1, ROWS, LANES), BF),
            pltpu.SemaphoreType.DMA((5,)),
            pltpu.SemaphoreType.DMA((intervals,)),
        ],
        compiler_params=pltpu.CompilerParams(vmem_limit_bytes=60 * MIB),
        name="pack",
    )(etype, *packing)

    received = [messages[0]] * space
    for turn in range(1, space):
        pairs = []
        for window in range(windows):
            for interval in range(intervals):
                host = host_of(window, interval, space, intervals)
                source = away(host, turn, window, space)
                pairs.append((window * space + source, window * space + host))
        received[turn] = lax.ppermute(messages[turn // stride], ("tm", "space"), pairs)

    table_shape = jax.ShapeDtypeStruct((ROWS + PROWS, (faces + 1) * ROWS), BF)
    fine_table, coarse_table, received[0] = pl.pallas_call(
        fold_kernel,
        out_shape=[table_shape] * 2 + [message_shape],
        in_specs=[VMEM] * 4,
        out_specs=[VMEM] * 3,
        scratch_shapes=[pltpu.VMEM((ROWS, (faces + 1) * ROWS), F32)],
        compiler_params=params,
        name="fold",
    )(block_inv, coarse_inv, coupling, messages[0])

    gather_shape = jax.ShapeDtypeStruct((space, 2 * LANES, (faces - PICKED) * LANES), BF)
    listing_shape = jax.ShapeDtypeStruct((space // 2, 2 * LANES, 2 * LANES), BF)
    aux_shape = jax.ShapeDtypeStruct((space, 8, LANES), F32)
    forcing_shape = jax.ShapeDtypeStruct((space, COARSEN, ROWS, LANES), BF)
    scratch = [
        pltpu.VMEM((space, ROWS, LANES), BF),
        pltpu.VMEM((space + 2, ROWS, LANES), BF),
        pltpu.VMEM((space // 2, (faces + 1) * ROWS, 2 * LANES), BF),
    ]
    residual, gather, listing, aux, whole_forcing, start = pl.pallas_call(
        functools.partial(fine_kernel, space, intervals, width, faces),
        out_shape=[state_shape, gather_shape, listing_shape, aux_shape, forcing_shape, state_shape],
        in_specs=[VMEM] * (space + 1),
        out_specs=[VMEM] * 6,
        scratch_shapes=scratch,
        compiler_params=params,
        name="fine",
    )(*received, fine_table)

    def from_earlier(value, by):
        pairs = []
        for number in range(by, windows * intervals):
            target = number // intervals
            source = (number - by) // intervals
            pairs.append(
                (
                    source * space + host_of(source, (number - by) % intervals, space, intervals),
                    target * space + host_of(target, number % intervals, space, intervals),
                )
            )
        return lax.ppermute(value, ("tm", "space"), pairs)

    def chain(kernel, number, terms, name):
        return pl.pallas_call(
            functools.partial(kernel, space, intervals, number, faces),
            out_shape=state_shape,
            in_specs=[VMEM] * (len(terms) + 4),
            out_specs=VMEM,
            scratch_shapes=scratch,
            compiler_params=params,
            name=name,
        )(*terms, coarse_table, gather, listing, aux)

    near = [from_earlier(residual, by) for by in range(intervals, 0, -1)]
    partial = chain(near_kernel, windows, near, "near")
    earlier, *inner = [
        from_earlier(partial, by * intervals) for by in range(windows - 1, 0, -1)
    ]
    earlier = chain(far_kernel, windows - 1, [earlier], "far")
    for index, term in enumerate(inner[:-1]):
        earlier = chain(far_kernel, windows - 2 - index, [earlier, term], "far")

    piece_shape = jax.ShapeDtypeStruct((COARSEN, width, LANES), BF)
    pieces = pl.pallas_call(
        functools.partial(final_kernel, space, intervals, width, faces),
        out_shape=[piece_shape] * space,
        in_specs=[VMEM] * (intervals + 10),
        out_specs=[VMEM] * space,
        scratch_shapes=[
            pltpu.VMEM((space, ROWS, LANES), BF),
            pltpu.VMEM((COARSEN, space, ROWS, LANES), BF),
        ]
        + scratch,
        compiler_params=params,
        name="final",
    )(
        *near,
        earlier,
        inner[-1],
        residual,
        start,
        whole_forcing,
        fine_table,
        coarse_table,
        gather,
        listing,
        aux,
    )

    returned = [pieces[0]] * space
    turns = distances(space, intervals)
    for turn in turns[1:]:
        pairs = []
        for window in range(windows):
            for interval in range(intervals):
                host = host_of(window, interval, space, intervals)
                target = away(host, turn, window, space)
                pairs.append((window * space + host, window * space + target))
        returned[turn] = lax.ppermute(pieces[turn], ("tm", "space"), pairs)

    return pl.pallas_call(
        functools.partial(gather_kernel, space, intervals),
        out_shape=jax.ShapeDtypeStruct(forcing.shape, BF),
        in_specs=[pl.BlockSpec(memory_space=pl.ANY)] * space,
        out_specs=VMEM,
        scratch_shapes=[pltpu.SemaphoreType.DMA((intervals,))],
        compiler_params=params,
        name="place",
    )(*[returned[turn] for turn in turns])


def solution(mesh):
    in_specs = (
        P(None, "space"),
        P("tm", None, "space"),
        P("space"),
        P(),
        P(),
        P(),
        P("space"),
        P("space"),
        P(None, "space"),
    )
    out_specs = P("tm", None, "space")
    return jax.shard_map(shards, mesh=mesh, in_specs=in_specs, out_specs=out_specs, check_vma=False)
```
